32 devices in a mesh: lat: 8 (over z, core), freq: 4 (over y, x).
Axes of the slice: x: 2, y: 2, z: 4, core: 2. Of those that a mesh axis runs over, the one named last changes fastest.
Arguments:
- wavefield: float32 [2, 8, 2048, 2048], P(None, 'freq', 'lat'), may hold values from -6 to 6
- source_field: float32 [2, 8, 2048, 2048], P(None, 'freq', 'lat'), may hold values from -6 to 6
- slowness: float32 [2048, 2048], P('lat', 'freq'), may hold values from 0.00015 to 0.00094
- freq_index: int32 [8], P('freq'), may hold values from 192 to 767, as said below
Outputs:
- next_field: float32 [2, 8, 2048, 2048], P(None, 'freq', 'lat')
- image: float32 [2048, 2048], P('lat', 'freq')
The draws below stay inside these ranges and needn't reach their ends.
Inputs may be any that keep to these rules, and one draw needn't show every extreme that they name: `freq_index`: distinct frequency indices.
All inputs are finite; a program needn't handle non-finite values.
Results may differ from the reference program's by a relative error of at most 0.00013.
Values sent between devices are 32-bit elements; how exact they have to be, the bound alone decides.
A program may use at most 128 MiB of HBM per device.

```python
import math
import jax
import jax.numpy as jnp
from jax import lax

NX = 2048
NY = 2048
BATCH = 8


def draw_slowness(key, part):
    rows = jnp.arange(NX, dtype=jnp.float32)[:, None] / (NX - 1)
    base = 1.0 / 4500.0 * (1.0 + 2.0 * rows)
    rough = jnp.exp(jax.random.uniform(key, (NX, NY), jnp.float32, jnp.log(0.7), jnp.log(1.4)))
    return base * rough


def draw_freq_index(key, part):
    first_key = jax.random.fold_in(key, 11)
    second_key = jax.random.fold_in(key, 23)
    middle = jax.random.permutation(first_key, 574)[:BATCH - 2] + 193
    values = jnp.concatenate([jnp.array([192, 767], jnp.int32), middle.astype(jnp.int32)])
    return jax.random.permutation(second_key, values).astype(jnp.int32)


def shard_levels(stream_key, shape, split, smallest, high):
    factor_of = 1.0
    for axis_at, blocks in split:
        heights = jax.random.uniform(jax.random.fold_in(jax.random.fold_in(stream_key, 6), axis_at), (blocks,), jnp.float32, smallest / len(split), high / len(split))
        factor_of = factor_of * jnp.repeat(jnp.exp(heights), shape[axis_at] // blocks).reshape((-1,) + (1,) * (len(shape) - 1 - axis_at))
    return factor_of


def noise(stream_key, extent, width, reach, shards=(), kind=jnp.bfloat16):
    level = shard_levels(stream_key, extent, shards, -0.22, 0.18) if shards else 1.0
    drawn = jax.random.normal(stream_key, extent, jnp.float32) * width * level
    return jnp.minimum(jnp.maximum(drawn, -reach), reach).astype(kind)


def setup_inputs(seed: int = 0) -> dict:
    streams_of = jax.random.split(jax.random.key(seed), 5)
    wavefield = noise(streams_of[0], (2, BATCH, NX, NY), 1.0, 6.0, ((1, 4), (2, 8)), jnp.float32)
    source_field = noise(streams_of[1], (2, BATCH, NX, NY), 1.0, 6.0, ((1, 4), (2, 8)), jnp.float32)
    slowness = draw_slowness(jax.random.fold_in(streams_of[4], 71), 0)
    freq_index = draw_freq_index(jax.random.fold_in(streams_of[4], 71), 0)
    return dict(wavefield=wavefield, source_field=source_field, slowness=slowness, freq_index=freq_index)


depth_step = 10.0
grid_step = 25.0
freq_step = 0.0625

def wave_numbers(count, float_type):
    indices = jnp.arange(count, dtype=jnp.int32)
    signed = jnp.where(indices < count // 2, indices, indices - count)
    return 2.0 * math.pi / (count * grid_step) * signed.astype(float_type)

def laplace_field(field):
    padded = jnp.pad(field, ((0, 0), (1, 1), (1, 1)))
    beside_all = padded[:, 2:, 1:-1] + padded[:, :-2, 1:-1] + padded[:, 1:-1, 2:] + padded[:, 1:-1, :-2]
    return beside_all - 4.0 * field

def reference(wavefield, source_field, slowness, freq_index):
    float_type = wavefield.dtype
    mean_slow = jnp.mean(slowness)
    angular = 2.0 * math.pi * freq_step * freq_index.astype(float_type)
    field = lax.complex(wavefield[0], wavefield[1])
    lens_angle = angular[:, None, None] * (slowness - mean_slow)[None] * depth_step
    field = field * lax.complex(jnp.cos(lens_angle), jnp.sin(lens_angle))
    spectrum = jnp.fft.fft2(field, axes=(1, 2))
    wave_x = wave_numbers(NX, float_type)
    wave_y = wave_numbers(NY, float_type)
    vertical = (angular * mean_slow)[:, None, None] ** 2 - wave_x[None, :, None] ** 2 - wave_y[None, None, :] ** 2
    damping = jnp.exp(-jnp.sqrt(jnp.maximum(-vertical, 0.0)) * depth_step)
    advance = jnp.sqrt(jnp.maximum(vertical, 0.0)) * depth_step
    spectrum = spectrum * lax.complex(damping * jnp.cos(advance), damping * jnp.sin(advance))
    field = jnp.fft.ifft2(spectrum, axes=(1, 2))
    real_part = jnp.real(field)
    imag_part = jnp.imag(field)
    lateral_gain = depth_step * (0.5 / (angular[:, None, None] * mean_slow) - 0.5 / (angular[:, None, None] * slowness[None])) / (grid_step * grid_step)
    new_real = real_part + lateral_gain * laplace_field(imag_part)
    new_imag = imag_part - lateral_gain * laplace_field(real_part)
    image = lax.optimization_barrier(jnp.sum(new_real * source_field[0] + new_imag * source_field[1], axis=0)) / math.sqrt(BATCH)
    return (jnp.stack([new_real, new_imag]), image)
```

```python
import functools
import math

import jax
import jax.numpy as jnp
import numpy as np
from jax import lax
from jax.experimental import pallas as pl
from jax.experimental.pallas import tpu as pltpu
from jax.sharding import PartitionSpec as P

depth_step = 10.0
grid_step = 25.0
freq_step = 0.0625
LANES = 128
CHUNK = 32
VMEM_BYTES = 60 * 1024 * 1024
MESH = pl.DeviceIdType.MESH


def dft_tables(sign):
    i = np.arange(LANES)
    ang = 2.0 * math.pi / LANES * ((i[:, None] * i[None, :]) % LANES)
    c, s = np.cos(ang), sign * np.sin(ang)
    return np.block([[c, s], [-s, c]])


def split_table(table):
    high = jnp.asarray(table.astype(np.float32)).astype(jnp.bfloat16)
    high64 = np.asarray(table.astype(np.float32).astype(jnp.bfloat16)).astype(np.float64)
    low = (table - high64).astype(np.float32).astype(jnp.bfloat16)
    return jnp.stack([high, jnp.asarray(low)])


def twiddle(count):
    factor = count // LANES
    k, n = np.arange(factor), np.arange(LANES)
    ang = 2.0 * math.pi / count * ((k[:, None] * n[None, :]) % count)
    return np.stack([np.cos(ang), np.sin(ang)]).astype(np.float32)


def fft_list(values, sign):
    count = len(values)
    if count == 1:
        return values
    even, odd = fft_list(values[0::2], sign), fft_list(values[1::2], sign)
    low, high = [], []
    for k in range(count // 2):
        (er, ei), (r, i) = even[k], odd[k]
        if k == 0:
            tr, ti = r, i
        elif 4 * k == count:
            tr, ti = (-i, r) if sign > 0 else (i, -r)
        else:
            c = math.cos(2.0 * math.pi * k / count)
            s = sign * math.sin(2.0 * math.pi * k / count)
            if abs(abs(c) - abs(s)) < 1e-9:
                h = math.sqrt(0.5)
                sc, ss = (1 if c > 0 else -1), (1 if s > 0 else -1)
                tr = h * (r - i) if sc * ss > 0 else h * (r + i)
                ti = h * (i + r) if sc * ss > 0 else h * (i - r)
                if sc < 0:
                    tr, ti = -tr, -ti
            else:
                tr, ti = c * r - s * i, c * i + s * r
        low.append((er + tr, ei + ti))
        high.append((er - tr, ei - ti))
    return low + high


def sin_cos(angle):
    turns = jnp.round(angle * (0.5 / math.pi))
    r = angle - turns * 6.28125 - turns * (2.0 * math.pi - 6.28125)
    r2 = r * r
    s = jnp.full_like(r, 1.0 / math.factorial(17))
    for n in range(15, 0, -2):
        s = s * r2 + ((-1) ** (n // 2)) / math.factorial(n)
    c = jnp.full_like(r, -1.0 / math.factorial(18))
    for n in range(16, -1, -2):
        c = c * r2 + ((-1) ** (n // 2)) / math.factorial(n)
    return s * r, c


def split(x):
    high = x.astype(jnp.bfloat16)
    return high, (x - high.astype(jnp.float32)).astype(jnp.bfloat16)


def dot(a, b):
    return jnp.dot(a, b, preferred_element_type=jnp.float32)


def flipped(index, mask, count):
    other, bit = index, 1
    while bit < count:
        if mask & bit:
            other = other + bit * (1 - 2 * ((index // bit) % 2))
        bit *= 2
    return other


def step_kernel(
    freq_ref, wave_hbm, src_hbm, slow_hbm, twx_hbm, tw_ref, m_fwd, m_both, m_inv,
    field_hbm, image_hbm,
    spec_out, spec_in, line_out, line_in, edge_out, edge_in, stat_out, stat_in,
    slow, terms, terms_in, zs, zc, ze, field, twx, wave, source, fresh, picture,
    wave_sem, source_sem, fresh_sem, image_sem, twx_sem, own_sem,
    slow_send, slow_recv, spec_send, spec_recv, spec_own, line_send, line_recv, line_own,
    edge_send, edge_recv, edge_own, stat_send, stat_recv, term_send, term_recv,
    *, batch_total,
):
    members, strips, rows_in, width = (spec_out.shape[i] for i in (0, 1, 3, 4))
    groups, part_width = slow.shape[0], slow.shape[2]
    full = strips * width
    factor = full // LANES
    count = rows_in * strips
    blocks = rows_in // CHUNK
    lane_blocks = width // LANES
    lat, fr = lax.axis_index("lat"), lax.axis_index("freq")
    lat_masks = sorted(range(1, strips), key=lambda m: -m)
    freq_masks = list(range(1, groups))

    def lat_peer(mask):
        return flipped(lat, mask, strips)

    def freq_peer(mask):
        return flipped(fr, mask, groups)

    def chunk_rows(i):
        return pl.ds(pl.multiple_of(i * CHUNK, CHUNK), CHUNK)

    def remote(a, b, send, recv, to):
        return pltpu.make_async_remote_copy(
            src_ref=a, dst_ref=b, send_sem=send, recv_sem=recv, device_id=to, device_id_type=MESH
        )

    def wave_copy(n):
        rows = chunk_rows(n % blocks)
        return pltpu.make_async_copy(
            wave_hbm.at[:, n // blocks, rows, :], wave.at[n % 2], wave_sem.at[n % 2]
        )

    def source_copy(n):
        rows = chunk_rows(n % blocks)
        return pltpu.make_async_copy(
            src_hbm.at[:, n // blocks, rows, :], source.at[n % 2], source_sem.at[n % 2]
        )

    def fresh_copy(n):
        rows = chunk_rows(n % blocks)
        return pltpu.make_async_copy(
            fresh.at[n % 2], field_hbm.at[:, n // blocks, rows, :], fresh_sem.at[n % 2]
        )

    own_slow = pltpu.make_async_copy(slow_hbm, slow.at[fr], own_sem)
    own_slow.start()
    wave_copy(0).start()
    source_copy(0).start()
    twx_copy = pltpu.make_async_copy(twx_hbm, twx, twx_sem)

    barrier = pltpu.get_barrier_semaphore()
    for mask in freq_masks:
        pl.semaphore_signal(barrier, inc=1, device_id=(lat, freq_peer(mask)), device_id_type=MESH)
    for mask in lat_masks:
        pl.semaphore_signal(barrier, inc=1, device_id=(lat_peer(mask), fr), device_id_type=MESH)
    pl.semaphore_wait(barrier, len(freq_masks) + len(lat_masks))

    def send_slow(i, carry):
        rows = chunk_rows(i)
        for mask in freq_masks:
            remote(
                slow_hbm.at[rows, :], slow.at[fr, rows, :], slow_send, slow_recv.at[i],
                (lat, freq_peer(mask)),
            ).start()
        return carry

    lax.fori_loop(0, blocks, send_slow, 0)
    own_slow.wait()

    def forward(n, carry):
        m, i = n // blocks, n % blocks
        rows = chunk_rows(i)

        @pl.when(n + 1 < members * blocks)
        def _():
            wave_copy(n + 1).start()

        @pl.when(n < blocks)
        def _():
            some = slow.at[pl.ds(0, groups - 1), rows, :]
            remote(some, some, slow_send, slow_recv.at[i], (lat, fr)).wait_recv()

        wave_copy(n).wait()
        scale = 2.0 * math.pi * freq_step * freq_ref[m].astype(jnp.float32) * depth_step
        slot = n % 2

        def tile(t, c0):
            r = pl.multiple_of(t * 8, 8)
            at_slow = pl.ds(pl.multiple_of(i * CHUNK + t * 8, 8), 8)
            cells = []
            for k in range(factor):
                at = k * LANES
                s = slow[at // part_width, at_slow, pl.ds(at % part_width, LANES)]
                sn, cs = sin_cos(s * scale)
                re = wave[slot, 0, pl.ds(r, 8), pl.ds(at, LANES)]
                im = wave[slot, 1, pl.ds(r, 8), pl.ds(at, LANES)]
                cells.append((re * cs - im * sn, re * sn + im * cs))
            for k, (re, im) in enumerate(fft_list(cells, -1.0)):
                if k:
                    c, s = tw_ref[0, pl.ds(k, 1), :], tw_ref[1, pl.ds(k, 1), :]
                    re, im = re * c + im * s, im * c - re * s
                zc[k, pl.ds(r, 8), pl.ds(0, LANES)] = re
                zc[k, pl.ds(r, 8), pl.ds(LANES, LANES)] = im
            return c0

        lax.fori_loop(0, CHUNK // 8, tile, 0)
        high, low = split(zc[...].reshape(factor * CHUNK, 2 * LANES))
        y = dot(high, m_fwd[0]) + (dot(low, m_fwd[0]) + dot(high, m_fwd[1]))
        y = y.reshape(factor, CHUNK, 2 * LANES)
        for k in range(factor):
            at = k * LANES
            cols = pl.ds(at % width, LANES)
            spec_out[m, at // width, 0, rows, cols] = y[k, :, :LANES]
            spec_out[m, at // width, 1, rows, cols] = y[k, :, LANES:]
        for mask in lat_masks:
            to = lat_peer(mask)
            remote(
                spec_out.at[m, to, :, rows, :], spec_in.at[m, lat, :, rows, :],
                spec_send.at[m], spec_recv.at[m, lat], (to, fr),
            ).start()
        pltpu.make_async_copy(
            spec_out.at[m, lat, :, rows, :], spec_in.at[m, lat, :, rows, :], spec_own.at[m]
        ).start()

        @pl.when(n == blocks - 1)
        def _():
            def add(t, sums):
                at_slow = pl.ds(pl.multiple_of(t * 8, 8), 8)
                for p in range(groups):
                    for at in range(0, part_width, LANES):
                        sums = sums + slow[p, at_slow, pl.ds(at, LANES)]
                return sums

            total = lax.fori_loop(0, rows_in // 8, add, jnp.zeros((8, LANES), jnp.float32))
            stat_out[...] = total
            stat_in[lat] = total
            for mask in lat_masks:
                remote(
                    stat_out, stat_in.at[lat], stat_send, stat_recv, (lat_peer(mask), fr)
                ).start()

        return carry

    lax.fori_loop(0, members * blocks, forward, 0)

    twx_copy.start()
    some = stat_in.at[pl.ds(0, strips - 1)]
    remote(some, some, stat_send, stat_recv, (lat, fr)).wait_recv()
    twx_copy.wait()
    mean = jnp.sum(stat_in[...]) * (1.0 / (count * full))

    def shift(m, carry):
        own = spec_in.at[m, lat]
        pltpu.make_async_copy(own, own, spec_own.at[m]).wait()
        for mask in lat_masks:
            peer = lat_peer(mask)
            whole_in = spec_in.at[m, peer]
            remote(whole_in, whole_in, spec_send.at[m], spec_recv.at[m, peer], (lat, fr)).wait_recv()

        def tile_in(t, c0):
            r = pl.multiple_of(t * 8, 8)
            for lane in range(0, width, LANES):
                lanes = pl.ds(lane, LANES)
                cells = []
                for n in range(factor):
                    at = n * LANES
                    rows = pl.ds(at % rows_in + r, 8)
                    cells.append(
                        (spec_in[m, at // rows_in, 0, rows, lanes],
                         spec_in[m, at // rows_in, 1, rows, lanes])
                    )
                for k, (re, im) in enumerate(fft_list(cells, -1.0)):
                    if k:
                        c, s = twx[0, k, pl.ds(r, 8), :], twx[1, k, pl.ds(r, 8), :]
                        re, im = re * c + im * s, im * c - re * s
                    zs[k, pl.ds(r, 8), lanes] = re
                    zs[k, pl.ds(LANES + r, 8), lanes] = im
            return c0

        lax.fori_loop(0, LANES // 8, tile_in, 0)

        angular_mean = 2.0 * math.pi * freq_step * freq_ref[m].astype(jnp.float32) * mean
        flat = angular_mean * depth_step
        place = lat * width + lax.broadcasted_iota(jnp.int32, (LANES, width), 1)
        index_y = place // LANES + factor * (place % LANES)
        signed_y = jnp.where(index_y < full // 2, index_y, index_y - full)
        wave_y = 2.0 * math.pi / (full * grid_step) * signed_y.astype(jnp.float32)
        rest = angular_mean * angular_mean - wave_y * wave_y
        row = lax.broadcasted_iota(jnp.int32, (LANES, width), 0)

        def product(k, c0):
            high, low = split(zs[k])
            y = dot(m_both[0], high) + (dot(m_both[0], low) + dot(m_both[1], high))
            index_x = k + factor * row
            signed_x = jnp.where(index_x < count // 2, index_x, index_x - count)
            wave_x = 2.0 * math.pi / (count * grid_step) * signed_x.astype(jnp.float32)
            vertical = rest - wave_x * wave_x
            size = jnp.sqrt(jnp.abs(vertical)) * depth_step
            damping = jnp.where(vertical < 0.0, jnp.exp(-size), 1.0) * (1.0 / (count * full))
            sn, cs = sin_cos(jnp.where(vertical > 0.0, size, 0.0) - flat)
            tr, ti = damping * cs, damping * sn
            re, im = y[:LANES], y[LANES:]
            z = jnp.concatenate([re * tr - im * ti, re * ti + im * tr], axis=0)
            high, low = split(z)
            zs[k] = dot(m_both[2], high) + (dot(m_both[2], low) + dot(m_both[3], high))
            return c0

        lax.fori_loop(0, factor, product, 0)

        def tile_out(t, c0):
            r = pl.multiple_of(t * 8, 8)
            for lane in range(0, width, LANES):
                lanes = pl.ds(lane, LANES)
                cells = []
                for k in range(factor):
                    re, im = zs[k, pl.ds(r, 8), lanes], zs[k, pl.ds(LANES + r, 8), lanes]
                    if k:
                        c, s = twx[0, k, pl.ds(r, 8), :], twx[1, k, pl.ds(r, 8), :]
                        re, im = re * c - im * s, im * c + re * s
                    cells.append((re, im))
                for n, (re, im) in enumerate(fft_list(cells, 1.0)):
                    at = n * LANES
                    rows = pl.ds(at % rows_in + r, 8)
                    line_out[m, at // rows_in, 0, rows, lanes] = re
                    line_out[m, at // rows_in, 1, rows, lanes] = im
            return c0

        lax.fori_loop(0, LANES // 8, tile_out, 0)

        for d in range(strips):
            for c in range(2):
                for e in range(2):
                    beside = d - 1 if e == 0 else d + 1
                    at_row = rows_in - 1 if e == 0 else 0
                    for b in range(lane_blocks):
                        if 0 <= beside < strips:
                            value = line_out[m, beside, c, pl.ds(at_row, 1), pl.ds(b * LANES, LANES)]
                        else:
                            value = jnp.zeros((1, LANES), jnp.float32)
                        at = (c * 2 + e) * lane_blocks + b
                        edge_out[m, d, pl.ds(at, 1), :] = value

        for mask in lat_masks:
            to = lat_peer(mask)
            remote(
                edge_out.at[m, to], edge_in.at[m, lat], edge_send.at[m], edge_recv.at[m], (to, fr)
            ).start()
        pltpu.make_async_copy(edge_out.at[m, lat], edge_in.at[m, lat], edge_own.at[m]).start()

        def send_lines(i, c0):
            rows = chunk_rows(i)
            for mask in lat_masks:
                to = lat_peer(mask)
                remote(
                    line_out.at[m, to, :, rows, :], line_in.at[m, lat, :, rows, :],
                    line_send.at[m], line_recv.at[m, i], (to, fr),
                ).start()
            pltpu.make_async_copy(
                line_out.at[m, lat, :, rows, :], line_in.at[m, lat, :, rows, :], line_own.at[m, i]
            ).start()
            return c0

        lax.fori_loop(0, blocks, send_lines, 0)
        return carry

    lax.fori_loop(0, members, shift, 0)

    def columns(z, rows):
        cells = []
        for k in range(factor):
            re, im = z[k, rows, pl.ds(0, LANES)], z[k, rows, pl.ds(LANES, LANES)]
            if k:
                c, s = tw_ref[0, pl.ds(k, 1), :], tw_ref[1, pl.ds(k, 1), :]
                re, im = re * c - im * s, im * c + re * s
            cells.append((re, im))
        return fft_list(cells, 1.0)

    def inverse_dot(x):
        high, low = split(x)
        return dot(high, m_inv[0]) + (dot(low, m_inv[0]) + dot(high, m_inv[1]))

    def edges(m):
        own = edge_in.at[m, lat]
        pltpu.make_async_copy(own, own, edge_own.at[m]).wait()
        some = edge_in.at[m, pl.ds(0, strips - 1)]
        remote(some, some, edge_send.at[m], edge_recv.at[m], (lat, fr)).wait_recv()
        ze[...] = jnp.zeros_like(ze)
        for k in range(factor):
            at = k * LANES
            b = (at % width) // LANES
            for c in range(2):
                for e in range(2):
                    row_at = (c * 2 + e) * lane_blocks + b
                    ze[k, pl.ds(e, 1), pl.ds(c * LANES, LANES)] = edge_in[
                        m, at // width, pl.ds(row_at, 1), :
                    ]
        y = inverse_dot(ze[...].reshape(factor * 8, 2 * LANES))
        ze[...] = y.reshape(factor, 8, 2 * LANES)
        for n, pair in enumerate(columns(ze, pl.ds(0, 8))):
            for c in range(2):
                field[c, pl.ds(7, 1), pl.ds(n * LANES, LANES)] = pair[c][0:1]
                field[c, pl.ds(8 + rows_in, 1), pl.ds(n * LANES, LANES)] = pair[c][1:2]

    def inverse_block(m, i):
        rows = chunk_rows(i)
        own = line_in.at[m, lat, :, rows, :]
        pltpu.make_async_copy(own, own, line_own.at[m, i]).wait()
        some = line_in.at[m, pl.ds(0, strips - 1), :, rows, :]
        remote(some, some, line_send.at[m], line_recv.at[m, i], (lat, fr)).wait_recv()
        parts = []
        for k in range(factor):
            at = k * LANES
            cols = pl.ds(at % width, LANES)
            parts.append(
                jnp.concatenate(
                    [line_in[m, at // width, 0, rows, cols], line_in[m, at // width, 1, rows, cols]],
                    axis=1,
                )
            )
        y = inverse_dot(jnp.concatenate(parts, axis=0))
        zc[...] = y.reshape(factor, CHUNK, 2 * LANES)

        def tile(t, c0):
            r = pl.multiple_of(t * 8, 8)
            at_field = pl.ds(pl.multiple_of(8 + i * CHUNK + t * 8, 8), 8)
            for n, pair in enumerate(columns(zc, pl.ds(r, 8))):
                for c in range(2):
                    field[c, at_field, pl.ds(n * LANES, LANES)] = pair[c]
            return c0

        lax.fori_loop(0, CHUNK // 8, tile, 0)

    column = lax.broadcasted_iota(jnp.int32, (CHUNK, full), 1)

    def stencil(m, i):
        n = m * blocks + i
        slot = n % 2
        rows = chunk_rows(i)

        @pl.when(n + 1 < members * blocks)
        def _():
            source_copy(n + 1).start()

        @pl.when(n >= 2)
        def _():
            fresh_copy(n - 2).wait()

        source_copy(n).wait()
        angular = 2.0 * math.pi * freq_step * freq_ref[m].astype(jnp.float32)
        ahead = 0.5 / (angular * mean)
        start = pl.multiple_of(i * CHUNK, CHUNK)
        centre, laplace = [], []
        for c in range(2):
            cells = field[c, pl.ds(start, CHUNK + 16), :]
            mid = cells[8 : 8 + CHUNK]
            up = pltpu.roll(cells, 1, 0)[8 : 8 + CHUNK]
            down = pltpu.roll(cells, CHUNK + 15, 0)[8 : 8 + CHUNK]
            left = jnp.where(column == 0, 0.0, pltpu.roll(mid, 1, 1))
            right = jnp.where(column == full - 1, 0.0, pltpu.roll(mid, full - 1, 1))
            centre.append(mid)
            laplace.append(up + down + left + right - 4.0 * mid)
        slow_rows = jnp.concatenate([slow[p, rows, :] for p in range(groups)], axis=1)
        gain = (ahead - 0.5 / (angular * slow_rows)) * (depth_step / (grid_step * grid_step))
        new_re = centre[0] + gain * laplace[1]
        new_im = centre[1] - gain * laplace[0]
        fresh[slot, 0] = new_re
        fresh[slot, 1] = new_im
        fresh_copy(n).start()
        term = (new_re * source[slot, 0] + new_im * source[slot, 1]) * (
            1.0 / math.sqrt(batch_total)
        )
        for p in range(groups):
            part = term[:, p * part_width : (p + 1) * part_width]

            @pl.when(m == 0)
            def _():
                terms[p, rows, :] = part

            @pl.when(m > 0)
            def _():
                terms[p, rows, :] = terms[p, rows, :] + part

        @pl.when(m == members - 1)
        def _():
            for mask in freq_masks:
                to = freq_peer(mask)
                remote(
                    terms.at[to, rows, :], terms_in.at[fr, rows, :], term_send, term_recv.at[i],
                    (lat, to),
                ).start()
            terms_in[fr, rows, :] = terms[fr, rows, :]

    def picture_block(i):
        rows = chunk_rows(i)
        some = terms_in.at[pl.ds(0, groups - 1), rows, :]
        remote(some, some, term_send, term_recv.at[i], (lat, fr)).wait_recv()
        total = terms_in[0, rows, :]
        for p in range(1, groups):
            total = total + terms_in[p, rows, :]
        picture[rows, :] = total
        pltpu.make_async_copy(picture.at[rows, :], image_hbm.at[rows, :], image_sem).start()

    def finish(n, carry):
        m, j = n // (blocks + 1), n % (blocks + 1)

        @pl.when(j == 0)
        def _():
            edges(m)

        @pl.when(j < blocks)
        def _():
            inverse_block(m, j)

        @pl.when(j > 0)
        def _():
            stencil(m, j - 1)

        @pl.when((m == members - 1) & (j > 2))
        def _():
            picture_block(j - 3)

        return carry

    lax.fori_loop(0, members * (blocks + 1), finish, 0)
    for i in range(max(blocks - 2, 0), blocks):
        picture_block(i)
    for n in range(members * blocks - 2, members * blocks):
        fresh_copy(n).wait()
    pltpu.make_async_copy(picture, image_hbm, image_sem).wait()

    some = slow.at[pl.ds(0, groups - 1)]
    remote(some, some, slow_send, slow_recv.at[0], (lat, fr)).wait_send()
    some = terms.at[pl.ds(0, groups - 1)]
    remote(some, some, term_send, term_recv.at[0], (lat, fr)).wait_send()
    some = stat_in.at[pl.ds(0, strips - 1)]
    remote(some, some, stat_send, stat_recv, (lat, fr)).wait_send()
    for m in range(members):
        some = spec_out.at[m, pl.ds(0, strips - 1)]
        remote(some, some, spec_send.at[m], spec_recv.at[m, 0], (lat, fr)).wait_send()
        some = line_out.at[m, pl.ds(0, strips - 1)]
        remote(some, some, line_send.at[m], line_recv.at[m, 0], (lat, fr)).wait_send()
        some = edge_out.at[m, pl.ds(0, strips - 1)]
        remote(some, some, edge_send.at[m], edge_recv.at[m], (lat, fr)).wait_send()


def local(wavefield, source_field, slowness, freq_index):
    _, members, rows, full = wavefield.shape
    strips, groups = lax.axis_size("lat"), lax.axis_size("freq")
    width = full // strips
    factor = full // LANES
    part_width = full // groups
    blocks = rows // CHUNK
    tw = twiddle(full)
    tw_row = jnp.asarray(tw)
    tw_x = jnp.asarray(np.ascontiguousarray(np.broadcast_to(tw[..., None], tw.shape + (LANES,))))
    right_fwd, right_inv = dft_tables(-1.0), dft_tables(1.0)
    m_fwd, m_inv = split_table(right_fwd), split_table(right_inv)
    m_both = jnp.concatenate(
        [split_table(np.ascontiguousarray(right_fwd.T)), split_table(np.ascontiguousarray(right_inv.T))]
    )
    edge_rows = max(8, 4 * width // LANES)
    anywhere = pl.BlockSpec(memory_space=pl.ANY)
    inside = pl.BlockSpec(memory_space=pltpu.VMEM)
    f32 = jnp.float32
    dma = pltpu.SemaphoreType.DMA
    return pl.pallas_call(
        functools.partial(step_kernel, batch_total=members * groups),
        in_specs=[pl.BlockSpec(memory_space=pltpu.SMEM)] + [anywhere] * 4 + [inside] * 4,
        out_specs=[anywhere, anywhere],
        out_shape=[
            jax.ShapeDtypeStruct((2, members, rows, full), f32),
            jax.ShapeDtypeStruct((rows, part_width), f32),
        ],
        scratch_shapes=[
            pltpu.VMEM((members, strips, 2, rows, width), f32),
            pltpu.VMEM((members, strips, 2, rows, width), f32),
            pltpu.VMEM((members, strips, 2, rows, width), f32),
            pltpu.VMEM((members, strips, 2, rows, width), f32),
            pltpu.VMEM((members, strips, edge_rows, LANES), f32),
            pltpu.VMEM((members, strips, edge_rows, LANES), f32),
            pltpu.VMEM((8, LANES), f32),
            pltpu.VMEM((strips, 8, LANES), f32),
            pltpu.VMEM((groups, rows, part_width), f32),
            pltpu.VMEM((groups, rows, part_width), f32),
            pltpu.VMEM((groups, rows, part_width), f32),
            pltpu.VMEM((factor, 2 * LANES, width), f32),
            pltpu.VMEM((factor, CHUNK, 2 * LANES), f32),
            pltpu.VMEM((factor, 8, 2 * LANES), f32),
            pltpu.VMEM((2, rows + 16, full), f32),
            pltpu.VMEM(tw_x.shape, f32),
            pltpu.VMEM((2, 2, CHUNK, full), f32),
            pltpu.VMEM((2, 2, CHUNK, full), f32),
            pltpu.VMEM((2, 2, CHUNK, full), f32),
            pltpu.VMEM((rows, part_width), f32),
            dma((2,)), dma((2,)), dma((2,)), dma, dma, dma,
            dma, dma((blocks,)),
            dma((members,)), dma((members, strips)), dma((members,)),
            dma((members,)), dma((members, blocks)), dma((members, blocks)),
            dma((members,)), dma((members,)), dma((members,)),
            dma, dma,
            dma, dma((blocks,)),
        ],
        compiler_params=pltpu.CompilerParams(
            collective_id=0, has_side_effects=True, vmem_limit_bytes=VMEM_BYTES
        ),
        cost_estimate=pl.CostEstimate(
            flops=13_000_000_000, bytes_accessed=26_000_000, transcendentals=0
        ),
        name="depth_step",
    )(freq_index, wavefield, source_field, slowness, tw_x, tw_row, m_fwd, m_both, m_inv)


def solution(mesh):
    return jax.shard_map(
        local,
        mesh=mesh,
        in_specs=(
            P(None, "freq", "lat", None),
            P(None, "freq", "lat", None),
            P("lat", "freq"),
            P("freq"),
        ),
        out_specs=(P(None, "freq", "lat", None), P("lat", "freq")),
        check_vma=False,
    )
```

```python
import functools
import math

import jax
import jax.numpy as jnp
import numpy as np
from jax import lax
from jax.experimental import pallas as pl
from jax.experimental.pallas import tpu as pltpu
from jax.sharding import PartitionSpec as P

depth_step = 10.0
grid_step = 25.0
freq_step = 0.0625
LANES = 128
CHUNK = 16
PIECE = 16
VMEM_BYTES = 52 * 1024 * 1024
SMALL_BYTES = 4 * 1024 * 1024
MESH = pl.DeviceIdType.MESH


def dft_tables(sign):
    i = np.arange(LANES)
    ang = 2.0 * math.pi / LANES * ((i[:, None] * i[None, :]) % LANES)
    c, s = np.cos(ang), sign * np.sin(ang)
    return np.block([[c, s], [-s, c]])


def split_table(table):
    high = jnp.asarray(table.astype(np.float32)).astype(jnp.bfloat16)
    high64 = np.asarray(table.astype(np.float32).astype(jnp.bfloat16)).astype(np.float64)
    low = (table - high64).astype(np.float32).astype(jnp.bfloat16)
    return jnp.stack([high, jnp.asarray(low)])


def twiddle(count):
    factor = count // LANES
    k, n = np.arange(factor), np.arange(LANES)
    ang = 2.0 * math.pi / count * ((k[:, None] * n[None, :]) % count)
    return np.stack([np.cos(ang), np.sin(ang)]).astype(np.float32)


def fft_list(values, sign):
    count = len(values)
    if count == 1:
        return values
    even, odd = fft_list(values[0::2], sign), fft_list(values[1::2], sign)
    low, high = [], []
    for k in range(count // 2):
        (er, ei), (r, i) = even[k], odd[k]
        if k == 0:
            tr, ti = r, i
        elif 4 * k == count:
            tr, ti = (-i, r) if sign > 0 else (i, -r)
        else:
            c = math.cos(2.0 * math.pi * k / count)
            s = sign * math.sin(2.0 * math.pi * k / count)
            if abs(abs(c) - abs(s)) < 1e-9:
                h = math.sqrt(0.5)
                sc, ss = (1 if c > 0 else -1), (1 if s > 0 else -1)
                tr = h * (r - i) if sc * ss > 0 else h * (r + i)
                ti = h * (i + r) if sc * ss > 0 else h * (i - r)
                if sc < 0:
                    tr, ti = -tr, -ti
            else:
                tr, ti = c * r - s * i, c * i + s * r
        low.append((er + tr, ei + ti))
        high.append((er - tr, ei - ti))
    return low + high


def sin_cos(angle):
    turns = jnp.round(angle * (0.5 / math.pi))
    r = angle - turns * 6.28125 - turns * (2.0 * math.pi - 6.28125)
    r2 = r * r
    s = jnp.full_like(r, 1.0 / math.factorial(17))
    for n in range(15, 0, -2):
        s = s * r2 + ((-1) ** (n // 2)) / math.factorial(n)
    c = jnp.full_like(r, -1.0 / math.factorial(18))
    for n in range(16, -1, -2):
        c = c * r2 + ((-1) ** (n // 2)) / math.factorial(n)
    return s * r, c


def split(x):
    high = x.astype(jnp.bfloat16)
    return high, (x - high.astype(jnp.float32)).astype(jnp.bfloat16)


def dot(a, b):
    return jnp.dot(a, b, preferred_element_type=jnp.float32)


def flipped(index, mask, count):
    other, bit = index, 1
    while bit < count:
        if mask & bit:
            other = other + bit * (1 - 2 * ((index // bit) % 2))
        bit *= 2
    return other


def step_kernel(
    freq_ref, wave_hbm, src_hbm, slow_hbm, twx_hbm, tw_ref, m_fwd, m_both, m_inv,
    fresh, terms_in,
    spec_out, spec_in, line_in, edge_out, edge_in, stat_out, stat_in,
    slow, terms, zs, zc, zp, ze, field, twx, wave, source,
    wave_sem, source_sem, twx_sem, own_sem,
    slow_send, slow_recv, spec_send, spec_recv, spec_own, line_send, line_recv, line_own,
    edge_send, edge_recv, edge_own, stat_send, stat_recv, term_send, term_recv,
    *, batch_total,
):
    members, strips, rows_in, width = (spec_out.shape[i] for i in (0, 1, 3, 4))
    groups, part_width = slow.shape[0], slow.shape[2]
    full = strips * width
    factor = full // LANES
    count = rows_in * strips
    blocks, pieces = rows_in // CHUNK, rows_in // PIECE
    lane_blocks = width // LANES
    lat, fr = lax.axis_index("lat"), lax.axis_index("freq")
    lat_masks = sorted(range(1, strips), key=lambda m: -m)
    freq_masks = list(range(1, groups))

    def lat_peer(mask):
        return flipped(lat, mask, strips)

    def freq_peer(mask):
        return flipped(fr, mask, groups)

    def chunk_rows(i):
        return pl.ds(pl.multiple_of(i * CHUNK, CHUNK), CHUNK)

    def piece_rows(i):
        return pl.ds(pl.multiple_of(i * PIECE, PIECE), PIECE)

    def remote(a, b, send, recv, to):
        return pltpu.make_async_remote_copy(
            src_ref=a, dst_ref=b, send_sem=send, recv_sem=recv, device_id=to, device_id_type=MESH
        )

    def wave_copy(n):
        rows = chunk_rows(n % blocks)
        return pltpu.make_async_copy(
            wave_hbm.at[:, n // blocks, rows, :], wave.at[n % 2], wave_sem.at[n % 2]
        )

    def source_copy(n):
        rows = piece_rows(n % pieces)
        return pltpu.make_async_copy(
            src_hbm.at[:, n // pieces, rows, :], source.at[n % 2], source_sem.at[n % 2]
        )

    own_slow = pltpu.make_async_copy(slow_hbm, slow.at[fr], own_sem)
    own_slow.start()
    wave_copy(0).start()
    source_copy(0).start()
    twx_copy = pltpu.make_async_copy(twx_hbm, twx, twx_sem)

    barrier = pltpu.get_barrier_semaphore()
    for mask in freq_masks:
        pl.semaphore_signal(barrier, inc=1, device_id=(lat, freq_peer(mask)), device_id_type=MESH)
    for mask in lat_masks:
        pl.semaphore_signal(barrier, inc=1, device_id=(lat_peer(mask), fr), device_id_type=MESH)
    pl.semaphore_wait(barrier, len(freq_masks) + len(lat_masks))

    def send_slow(i, carry):
        rows = chunk_rows(i)
        for mask in freq_masks:
            remote(
                slow_hbm.at[rows, :], slow.at[fr, rows, :], slow_send, slow_recv.at[i],
                (lat, freq_peer(mask)),
            ).start()
        return carry

    lax.fori_loop(0, blocks, send_slow, 0)
    own_slow.wait()

    def forward(n, carry):
        m, i = n // blocks, n % blocks
        rows = chunk_rows(i)

        @pl.when(n + 1 < members * blocks)
        def _():
            wave_copy(n + 1).start()

        @pl.when(n < blocks)
        def _():
            some = slow.at[pl.ds(0, groups - 1), rows, :]
            remote(some, some, slow_send, slow_recv.at[i], (lat, fr)).wait_recv()

        wave_copy(n).wait()
        scale = 2.0 * math.pi * freq_step * freq_ref[m].astype(jnp.float32) * depth_step
        slot = n % 2

        def tile(t, c0):
            r = pl.multiple_of(t * 8, 8)
            at_slow = pl.ds(pl.multiple_of(i * CHUNK + t * 8, 8), 8)
            cells = []
            for k in range(factor):
                at = k * LANES
                s = slow[at // part_width, at_slow, pl.ds(at % part_width, LANES)]
                sn, cs = sin_cos(s * scale)
                re = wave[slot, 0, pl.ds(r, 8), pl.ds(at, LANES)]
                im = wave[slot, 1, pl.ds(r, 8), pl.ds(at, LANES)]
                cells.append((re * cs - im * sn, re * sn + im * cs))
            for k, (re, im) in enumerate(fft_list(cells, -1.0)):
                if k:
                    c, s = tw_ref[0, pl.ds(k, 1), :], tw_ref[1, pl.ds(k, 1), :]
                    re, im = re * c + im * s, im * c - re * s
                zc[k, pl.ds(r, 8), pl.ds(0, LANES)] = re
                zc[k, pl.ds(r, 8), pl.ds(LANES, LANES)] = im
            return c0

        lax.fori_loop(0, CHUNK // 8, tile, 0)
        high, low = split(zc[...].reshape(factor * CHUNK, 2 * LANES))
        y = dot(high, m_fwd[0]) + (dot(low, m_fwd[0]) + dot(high, m_fwd[1]))
        y = y.reshape(factor, CHUNK, 2 * LANES)
        for k in range(factor):
            at = k * LANES
            cols = pl.ds(at % width, LANES)
            spec_out[m, at // width, 0, rows, cols] = y[k, :, :LANES]
            spec_out[m, at // width, 1, rows, cols] = y[k, :, LANES:]
        for mask in lat_masks:
            to = lat_peer(mask)
            remote(
                spec_out.at[m, to, :, rows, :], spec_in.at[m, lat, :, rows, :],
                spec_send.at[m], spec_recv.at[m, lat], (to, fr),
            ).start()
        pltpu.make_async_copy(
            spec_out.at[m, lat, :, rows, :], spec_in.at[m, lat, :, rows, :], spec_own.at[m]
        ).start()

        @pl.when(n == blocks - 1)
        def _():
            def add(t, sums):
                at_slow = pl.ds(pl.multiple_of(t * 8, 8), 8)
                for p in range(groups):
                    for at in range(0, part_width, LANES):
                        sums = sums + slow[p, at_slow, pl.ds(at, LANES)]
                return sums

            total = lax.fori_loop(0, rows_in // 8, add, jnp.zeros((8, LANES), jnp.float32))
            stat_out[...] = total
            stat_in[lat] = total
            for mask in lat_masks:
                remote(
                    stat_out, stat_in.at[lat], stat_send, stat_recv, (lat_peer(mask), fr)
                ).start()

        return carry

    lax.fori_loop(0, members * blocks, forward, 0)

    twx_copy.start()
    some = stat_in.at[pl.ds(0, strips - 1)]
    remote(some, some, stat_send, stat_recv, (lat, fr)).wait_recv()
    twx_copy.wait()
    mean = jnp.sum(stat_in[...]) * (1.0 / (count * full))

    def shift(m, carry):
        own = spec_in.at[m, lat]
        pltpu.make_async_copy(own, own, spec_own.at[m]).wait()
        for mask in lat_masks:
            peer = lat_peer(mask)
            whole_in = spec_in.at[m, peer]
            remote(whole_in, whole_in, spec_send.at[m], spec_recv.at[m, peer], (lat, fr)).wait_recv()

        def tile_in(t, c0):
            r = pl.multiple_of(t * 8, 8)
            for lane in range(0, width, LANES):
                lanes = pl.ds(lane, LANES)
                cells = []
                for n in range(factor):
                    at = n * LANES
                    rows = pl.ds(at % rows_in + r, 8)
                    cells.append(
                        (spec_in[m, at // rows_in, 0, rows, lanes],
                         spec_in[m, at // rows_in, 1, rows, lanes])
                    )
                for k, (re, im) in enumerate(fft_list(cells, -1.0)):
                    if k:
                        c, s = twx[0, k, pl.ds(r, 8), :], twx[1, k, pl.ds(r, 8), :]
                        re, im = re * c + im * s, im * c - re * s
                    zs[k, pl.ds(r, 8), lanes] = re
                    zs[k, pl.ds(LANES + r, 8), lanes] = im
            return c0

        lax.fori_loop(0, LANES // 8, tile_in, 0)

        angular_mean = 2.0 * math.pi * freq_step * freq_ref[m].astype(jnp.float32) * mean
        flat = angular_mean * depth_step
        place = lat * width + lax.broadcasted_iota(jnp.int32, (LANES, width), 1)
        index_y = place // LANES + factor * (place % LANES)
        signed_y = jnp.where(index_y < full // 2, index_y, index_y - full)
        wave_y = 2.0 * math.pi / (full * grid_step) * signed_y.astype(jnp.float32)
        rest = angular_mean * angular_mean - wave_y * wave_y
        row = lax.broadcasted_iota(jnp.int32, (LANES, width), 0)

        def product(k, c0):
            high, low = split(zs[k])
            y = dot(m_both[0], high) + (dot(m_both[0], low) + dot(m_both[1], high))
            index_x = k + factor * row
            signed_x = jnp.where(index_x < count // 2, index_x, index_x - count)
            wave_x = 2.0 * math.pi / (count * grid_step) * signed_x.astype(jnp.float32)
            vertical = rest - wave_x * wave_x
            size = jnp.sqrt(jnp.abs(vertical)) * depth_step
            damping = jnp.where(vertical < 0.0, jnp.exp(-size), 1.0) * (1.0 / (count * full))
            sn, cs = sin_cos(jnp.where(vertical > 0.0, size, 0.0) - flat)
            tr, ti = damping * cs, damping * sn
            re, im = y[:LANES], y[LANES:]
            z = jnp.concatenate([re * tr - im * ti, re * ti + im * tr], axis=0)
            high, low = split(z)
            zs[k] = dot(m_both[2], high) + (dot(m_both[2], low) + dot(m_both[3], high))
            return c0

        lax.fori_loop(0, factor, product, 0)
        some = spec_out.at[m, pl.ds(0, strips - 1)]
        remote(some, some, spec_send.at[m], spec_recv.at[m, 0], (lat, fr)).wait_send()

        def tile_out(t, c0):
            r = pl.multiple_of(t * 8, 8)
            for lane in range(0, width, LANES):
                lanes = pl.ds(lane, LANES)
                cells = []
                for k in range(factor):
                    re, im = zs[k, pl.ds(r, 8), lanes], zs[k, pl.ds(LANES + r, 8), lanes]
                    if k:
                        c, s = twx[0, k, pl.ds(r, 8), :], twx[1, k, pl.ds(r, 8), :]
                        re, im = re * c - im * s, im * c + re * s
                    cells.append((re, im))
                for n, (re, im) in enumerate(fft_list(cells, 1.0)):
                    at = n * LANES
                    rows = pl.ds(at % rows_in + r, 8)
                    spec_out[m, at // rows_in, 0, rows, lanes] = re
                    spec_out[m, at // rows_in, 1, rows, lanes] = im
            return c0

        lax.fori_loop(0, LANES // 8, tile_out, 0)

        for d in range(strips):
            for c in range(2):
                for e in range(2):
                    beside = d - 1 if e == 0 else d + 1
                    at_row = rows_in - 1 if e == 0 else 0
                    for b in range(lane_blocks):
                        if 0 <= beside < strips:
                            value = spec_out[m, beside, c, pl.ds(at_row, 1), pl.ds(b * LANES, LANES)]
                        else:
                            value = jnp.zeros((1, LANES), jnp.float32)
                        at = (c * 2 + e) * lane_blocks + b
                        edge_out[m, d, pl.ds(at, 1), :] = value

        for mask in lat_masks:
            to = lat_peer(mask)
            remote(
                edge_out.at[m, to], edge_in.at[m, lat], edge_send.at[m], edge_recv.at[m], (to, fr)
            ).start()
        pltpu.make_async_copy(edge_out.at[m, lat], edge_in.at[m, lat], edge_own.at[m]).start()

        def send_lines(i, c0):
            rows = piece_rows(i)
            for mask in lat_masks:
                to = lat_peer(mask)
                remote(
                    spec_out.at[m, to, :, rows, :], line_in.at[m, lat, :, rows, :],
                    line_send.at[m], line_recv.at[m, i], (to, fr),
                ).start()
            pltpu.make_async_copy(
                spec_out.at[m, lat, :, rows, :], line_in.at[m, lat, :, rows, :], line_own.at[m, i]
            ).start()
            return c0

        lax.fori_loop(0, pieces, send_lines, 0)
        return carry

    lax.fori_loop(0, members, shift, 0)

    def columns(z, rows):
        cells = []
        for k in range(factor):
            re, im = z[k, rows, pl.ds(0, LANES)], z[k, rows, pl.ds(LANES, LANES)]
            if k:
                c, s = tw_ref[0, pl.ds(k, 1), :], tw_ref[1, pl.ds(k, 1), :]
                re, im = re * c - im * s, im * c + re * s
            cells.append((re, im))
        return fft_list(cells, 1.0)

    def inverse_dot(x):
        high, low = split(x)
        return dot(high, m_inv[0]) + (dot(low, m_inv[0]) + dot(high, m_inv[1]))

    def edges(m):
        own = edge_in.at[m, lat]
        pltpu.make_async_copy(own, own, edge_own.at[m]).wait()
        some = edge_in.at[m, pl.ds(0, strips - 1)]
        remote(some, some, edge_send.at[m], edge_recv.at[m], (lat, fr)).wait_recv()
        ze[...] = jnp.zeros_like(ze)
        for k in range(factor):
            at = k * LANES
            b = (at % width) // LANES
            for c in range(2):
                for e in range(2):
                    row_at = (c * 2 + e) * lane_blocks + b
                    ze[k, pl.ds(e, 1), pl.ds(c * LANES, LANES)] = edge_in[
                        m, at // width, pl.ds(row_at, 1), :
                    ]
        y = inverse_dot(ze[...].reshape(factor * 8, 2 * LANES))
        ze[...] = y.reshape(factor, 8, 2 * LANES)
        for n, pair in enumerate(columns(ze, pl.ds(0, 8))):
            for c in range(2):
                field[c, pl.ds(7, 1), pl.ds(n * LANES, LANES)] = pair[c][0:1]
                field[c, pl.ds(8 + rows_in, 1), pl.ds(n * LANES, LANES)] = pair[c][1:2]

    def inverse_block(m, i):
        rows = piece_rows(i)
        own = line_in.at[m, lat, :, rows, :]
        pltpu.make_async_copy(own, own, line_own.at[m, i]).wait()
        some = line_in.at[m, pl.ds(0, strips - 1), :, rows, :]
        remote(some, some, line_send.at[m], line_recv.at[m, i], (lat, fr)).wait_recv()
        parts = []
        for k in range(factor):
            at = k * LANES
            cols = pl.ds(at % width, LANES)
            parts.append(
                jnp.concatenate(
                    [line_in[m, at // width, 0, rows, cols], line_in[m, at // width, 1, rows, cols]],
                    axis=1,
                )
            )
        y = inverse_dot(jnp.concatenate(parts, axis=0))
        zp[...] = y.reshape(factor, PIECE, 2 * LANES)

        def tile(t, c0):
            r = pl.multiple_of(t * 8, 8)
            at_field = pl.ds(pl.multiple_of(8 + i * PIECE + t * 8, 8), 8)
            for n, pair in enumerate(columns(zp, pl.ds(r, 8))):
                for c in range(2):
                    field[c, at_field, pl.ds(n * LANES, LANES)] = pair[c]
            return c0

        lax.fori_loop(0, PIECE // 8, tile, 0)

    column = lax.broadcasted_iota(jnp.int32, (PIECE, full), 1)

    def stencil(m, i):
        n = m * pieces + i
        slot = n % 2
        rows = piece_rows(i)

        @pl.when(n + 1 < members * pieces)
        def _():
            source_copy(n + 1).start()

        source_copy(n).wait()
        angular = 2.0 * math.pi * freq_step * freq_ref[m].astype(jnp.float32)
        ahead = 0.5 / (angular * mean)
        start = pl.multiple_of(i * PIECE, PIECE)
        centre, laplace = [], []
        for c in range(2):
            cells = field[c, pl.ds(start, PIECE + 16), :]
            mid = cells[8 : 8 + PIECE]
            up = pltpu.roll(cells, 1, 0)[8 : 8 + PIECE]
            down = pltpu.roll(cells, PIECE + 15, 0)[8 : 8 + PIECE]
            left = jnp.where(column == 0, 0.0, pltpu.roll(mid, 1, 1))
            right = jnp.where(column == full - 1, 0.0, pltpu.roll(mid, full - 1, 1))
            centre.append(mid)
            laplace.append(up + down + left + right - 4.0 * mid)
        slow_rows = jnp.concatenate([slow[p, rows, :] for p in range(groups)], axis=1)
        gain = (ahead - 0.5 / (angular * slow_rows)) * (depth_step / (grid_step * grid_step))
        new_re = centre[0] + gain * laplace[1]
        new_im = centre[1] - gain * laplace[0]
        fresh[0, m, rows, :] = new_re
        fresh[1, m, rows, :] = new_im
        term = (new_re * source[slot, 0] + new_im * source[slot, 1]) * (
            1.0 / math.sqrt(batch_total)
        )
        for p in range(groups):
            part = term[:, p * part_width : (p + 1) * part_width]

            @pl.when(m == 0)
            def _():
                terms[p, rows, :] = part

            @pl.when(m > 0)
            def _():
                terms[p, rows, :] = terms[p, rows, :] + part

        @pl.when(m == members - 1)
        def _():
            for mask in freq_masks:
                to = freq_peer(mask)
                remote(
                    terms.at[to, rows, :], terms_in.at[fr, rows, :], term_send, term_recv,
                    (lat, to),
                ).start()
            terms_in[fr, rows, :] = terms[fr, rows, :]

    def finish(n, carry):
        m, j = n // (pieces + 1), n % (pieces + 1)

        @pl.when(j == 0)
        def _():
            edges(m)

        @pl.when(j < pieces)
        def _():
            inverse_block(m, j)

        @pl.when(j > 0)
        def _():
            stencil(m, j - 1)

        return carry

    lax.fori_loop(0, members * (pieces + 1), finish, 0)
    some = slow.at[pl.ds(0, groups - 1)]
    remote(some, some, slow_send, slow_recv.at[0], (lat, fr)).wait_send()
    some = terms.at[pl.ds(0, groups - 1)]
    remote(some, some, term_send, term_recv, (lat, fr)).wait()
    some = stat_in.at[pl.ds(0, strips - 1)]
    remote(some, some, stat_send, stat_recv, (lat, fr)).wait_send()
    for m in range(members):
        some = spec_out.at[m, pl.ds(0, strips - 1)]
        remote(some, some, line_send.at[m], line_recv.at[m, 0], (lat, fr)).wait_send()
        some = edge_out.at[m, pl.ds(0, strips - 1)]
        remote(some, some, edge_send.at[m], edge_recv.at[m], (lat, fr)).wait_send()


def write_kernel(fresh, terms, field_hbm, image, sem):
    copies = [
        pltpu.make_async_copy(fresh.at[c, m], field_hbm.at[c, m], sem)
        for c in range(fresh.shape[0])
        for m in range(fresh.shape[1])
    ]
    for copy in copies:
        copy.start()
    total = terms[0]
    for p in range(1, terms.shape[0]):
        total = total + terms[p]
    image[...] = total
    pltpu.make_async_copy(fresh, field_hbm, sem).wait()


def local(wavefield, source_field, slowness, freq_index):
    _, members, rows, full = wavefield.shape
    strips, groups = lax.axis_size("lat"), lax.axis_size("freq")
    width = full // strips
    factor = full // LANES
    part_width = full // groups
    blocks, pieces = rows // CHUNK, rows // PIECE
    tw = twiddle(full)
    tw_row = jnp.asarray(tw)
    tw_x = jnp.asarray(np.ascontiguousarray(np.broadcast_to(tw[..., None], tw.shape + (LANES,))))
    right_fwd, right_inv = dft_tables(-1.0), dft_tables(1.0)
    m_fwd, m_inv = split_table(right_fwd), split_table(right_inv)
    m_both = jnp.concatenate(
        [split_table(np.ascontiguousarray(right_fwd.T)), split_table(np.ascontiguousarray(right_inv.T))]
    )
    edge_rows = max(8, 4 * width // LANES)
    far = pl.BlockSpec(memory_space=pltpu.HBM)
    anywhere = pl.BlockSpec(memory_space=pl.ANY)
    inside = pl.BlockSpec(memory_space=pltpu.VMEM)
    f32 = jnp.float32
    dma = pltpu.SemaphoreType.DMA
    fresh, terms = pl.pallas_call(
        functools.partial(step_kernel, batch_total=members * groups),
        in_specs=[pl.BlockSpec(memory_space=pltpu.SMEM)] + [far] * 4 + [inside] * 4,
        out_specs=[inside, inside],
        out_shape=[
            pltpu.VMEM((2, members, rows, full), f32),
            pltpu.VMEM((groups, rows, part_width), f32),
        ],
        scratch_shapes=[
            pltpu.VMEM((members, strips, 2, rows, width), f32),
            pltpu.VMEM((members, strips, 2, rows, width), f32),
            pltpu.VMEM((members, strips, 2, rows, width), f32),
            pltpu.VMEM((members, strips, edge_rows, LANES), f32),
            pltpu.VMEM((members, strips, edge_rows, LANES), f32),
            pltpu.VMEM((8, LANES), f32),
            pltpu.VMEM((strips, 8, LANES), f32),
            pltpu.VMEM((groups, rows, part_width), f32),
            pltpu.VMEM((groups, rows, part_width), f32),
            pltpu.VMEM((factor, 2 * LANES, width), f32),
            pltpu.VMEM((factor, CHUNK, 2 * LANES), f32),
            pltpu.VMEM((factor, PIECE, 2 * LANES), f32),
            pltpu.VMEM((factor, 8, 2 * LANES), f32),
            pltpu.VMEM((2, rows + 16, full), f32),
            pltpu.VMEM(tw_x.shape, f32),
            pltpu.VMEM((2, 2, CHUNK, full), f32),
            pltpu.VMEM((2, 2, PIECE, full), f32),
            dma((2,)), dma((2,)), dma, dma,
            dma, dma((blocks,)),
            dma((members,)), dma((members, strips)), dma((members,)),
            dma((members,)), dma((members, pieces)), dma((members, pieces)),
            dma((members,)), dma((members,)), dma((members,)),
            dma, dma,
            dma, dma,
        ],
        compiler_params=pltpu.CompilerParams(
            collective_id=0, has_side_effects=True, vmem_limit_bytes=VMEM_BYTES
        ),
        cost_estimate=pl.CostEstimate(
            flops=13_000_000_000, bytes_accessed=26_000_000, transcendentals=0
        ),
        name="depth_step",
    )(freq_index, wavefield, source_field, slowness, tw_x, tw_row, m_fwd, m_both, m_inv)
    return pl.pallas_call(
        write_kernel,
        in_specs=[inside, inside],
        out_specs=[anywhere, inside],
        out_shape=[
            jax.ShapeDtypeStruct((2, members, rows, full), f32),
            jax.ShapeDtypeStruct((rows, part_width), f32),
        ],
        scratch_shapes=[dma],
        compiler_params=pltpu.CompilerParams(vmem_limit_bytes=SMALL_BYTES),
        cost_estimate=pl.CostEstimate(flops=400_000, bytes_accessed=8_400_000, transcendentals=0),
        name="write_out",
    )(fresh, terms)


def solution(mesh):
    return jax.shard_map(
        local,
        mesh=mesh,
        in_specs=(
            P(None, "freq", "lat", None),
            P(None, "freq", "lat", None),
            P("lat", "freq"),
            P("freq"),
        ),
        out_specs=(P(None, "freq", "lat", None), P("lat", "freq")),
        check_vma=False,
    )
```

```python
import functools
import math

import jax
import jax.numpy as jnp
import numpy as np
from jax import lax
from jax.experimental import pallas as pl
from jax.experimental.pallas import tpu as pltpu
from jax.sharding import PartitionSpec as P

depth_step = 10.0
grid_step = 25.0
freq_step = 0.0625
LANES = 128
CHUNK = 8
PIECE = 8
AHEAD = 2
VMEM_BYTES = 52 * 1024 * 1024
SMALL_BYTES = 4 * 1024 * 1024
MESH = pl.DeviceIdType.MESH


def dft_tables(sign):
    i = np.arange(LANES)
    ang = 2.0 * math.pi / LANES * ((i[:, None] * i[None, :]) % LANES)
    c, s = np.cos(ang), sign * np.sin(ang)
    return np.block([[c, s], [-s, c]])


def split_table(table):
    high = jnp.asarray(table.astype(np.float32)).astype(jnp.bfloat16)
    high64 = np.asarray(table.astype(np.float32).astype(jnp.bfloat16)).astype(np.float64)
    low = (table - high64).astype(np.float32).astype(jnp.bfloat16)
    return jnp.stack([high, jnp.asarray(low)])


def twiddle(count):
    factor = count // LANES
    k, n = np.arange(factor), np.arange(LANES)
    ang = 2.0 * math.pi / count * ((k[:, None] * n[None, :]) % count)
    return np.stack([np.cos(ang), np.sin(ang)]).astype(np.float32)


def fft_list(values, sign):
    count = len(values)
    if count == 1:
        return values
    even, odd = fft_list(values[0::2], sign), fft_list(values[1::2], sign)
    low, high = [], []
    for k in range(count // 2):
        (er, ei), (r, i) = even[k], odd[k]
        if k == 0:
            tr, ti = r, i
        elif 4 * k == count:
            tr, ti = (-i, r) if sign > 0 else (i, -r)
        else:
            c = math.cos(2.0 * math.pi * k / count)
            s = sign * math.sin(2.0 * math.pi * k / count)
            if abs(abs(c) - abs(s)) < 1e-9:
                h = math.sqrt(0.5)
                sc, ss = (1 if c > 0 else -1), (1 if s > 0 else -1)
                tr = h * (r - i) if sc * ss > 0 else h * (r + i)
                ti = h * (i + r) if sc * ss > 0 else h * (i - r)
                if sc < 0:
                    tr, ti = -tr, -ti
            else:
                tr, ti = c * r - s * i, c * i + s * r
        low.append((er + tr, ei + ti))
        high.append((er - tr, ei - ti))
    return low + high


def sin_cos(angle):
    turns = jnp.round(angle * (0.5 / math.pi))
    r = angle - turns * 6.28125 - turns * (2.0 * math.pi - 6.28125)
    r2 = r * r
    s = jnp.full_like(r, 1.0 / math.factorial(17))
    for n in range(15, 0, -2):
        s = s * r2 + ((-1) ** (n // 2)) / math.factorial(n)
    c = jnp.full_like(r, -1.0 / math.factorial(18))
    for n in range(16, -1, -2):
        c = c * r2 + ((-1) ** (n // 2)) / math.factorial(n)
    return s * r, c


def split(x):
    high = x.astype(jnp.bfloat16)
    return high, (x - high.astype(jnp.float32)).astype(jnp.bfloat16)


def dot(a, b):
    return jnp.dot(a, b, preferred_element_type=jnp.float32)


def flipped(index, mask, count):
    other, bit = index, 1
    while bit < count:
        if mask & bit:
            other = other + bit * (1 - 2 * ((index // bit) % 2))
        bit *= 2
    return other


def step_kernel(
    freq_ref, wave_hbm, src_hbm, slow_hbm, twx_hbm, tw_hbm, fwd_hbm, both_hbm, inv_hbm,
    fresh, terms_in,
    spec_out, spec_in, line_in, edge_out, edge_in, stat_out, stat_in,
    slow, terms, zs, zc, zp, ze, field, wave, source,
    twx, tw_ref, m_fwd, m_both, m_inv,
    wave_sem, source_sem, early_sem, late_sem, own_sem,
    slow_send, slow_recv, spec_send, spec_recv, spec_own, line_send, line_recv, line_own,
    edge_send, edge_recv, edge_own, stat_send, stat_recv, term_send, term_recv,
    *, batch_total,
):
    members, strips, rows_in, width = (spec_out.shape[i] for i in (0, 1, 3, 4))
    groups, part_width = slow.shape[0], slow.shape[2]
    full = strips * width
    factor = full // LANES
    count = rows_in * strips
    blocks, pieces = rows_in // CHUNK, rows_in // PIECE
    lane_blocks = width // LANES
    lat, fr = lax.axis_index("lat"), lax.axis_index("freq")
    lat_masks = sorted(range(1, strips), key=lambda m: -m)
    freq_masks = list(range(1, groups))

    def lat_peer(mask):
        return flipped(lat, mask, strips)

    def freq_peer(mask):
        return flipped(fr, mask, groups)

    def chunk_rows(i):
        return pl.ds(pl.multiple_of(i * CHUNK, CHUNK), CHUNK)

    def piece_rows(i):
        return pl.ds(pl.multiple_of(i * PIECE, PIECE), PIECE)

    def remote(a, b, send, recv, to):
        return pltpu.make_async_remote_copy(
            src_ref=a, dst_ref=b, send_sem=send, recv_sem=recv, device_id=to, device_id_type=MESH
        )

    def wave_copy(n):
        rows = chunk_rows(n % blocks)
        return pltpu.make_async_copy(
            wave_hbm.at[:, n // blocks, rows, :], wave.at[n % 2], wave_sem.at[n % 2]
        )

    def source_copy(n):
        rows = piece_rows(n % pieces)
        return pltpu.make_async_copy(
            src_hbm.at[:, n // pieces, rows, :], source.at[n % 2], source_sem.at[n % 2]
        )

    barrier = pltpu.get_barrier_semaphore()
    for mask in freq_masks:
        pl.semaphore_signal(barrier, inc=1, device_id=(lat, freq_peer(mask)), device_id_type=MESH)
    for mask in lat_masks:
        pl.semaphore_signal(barrier, inc=1, device_id=(lat_peer(mask), fr), device_id_type=MESH)

    own_slow = pltpu.make_async_copy(slow_hbm, slow.at[fr], own_sem)
    own_slow.start()
    wave_copy(0).start()
    early = [
        pltpu.make_async_copy(a, b, early_sem.at[i])
        for i, (a, b) in enumerate(((tw_hbm, tw_ref), (fwd_hbm, m_fwd)))
    ]
    late = [
        pltpu.make_async_copy(a, b, late_sem.at[i])
        for i, (a, b) in enumerate(((twx_hbm, twx), (both_hbm, m_both), (inv_hbm, m_inv)))
    ]
    for copy in early:
        copy.start()
    pl.semaphore_wait(barrier, len(freq_masks) + len(lat_masks))

    def send_slow(i, carry):
        rows = chunk_rows(i)
        for mask in freq_masks:
            remote(
                slow.at[fr, rows, :], slow.at[fr, rows, :], slow_send, slow_recv.at[i],
                (lat, freq_peer(mask)),
            ).start()
        return carry

    own_slow.wait()
    lax.fori_loop(0, min(AHEAD, blocks), send_slow, 0)
    for copy in early:
        copy.wait()

    def forward(n, carry):
        m, i = n // blocks, n % blocks
        rows = chunk_rows(i)

        @pl.when(n + 1 < members * blocks)
        def _():
            wave_copy(n + 1).start()

        @pl.when(n + AHEAD < blocks)
        def _():
            send_slow(n + AHEAD, 0)

        @pl.when(n < blocks)
        def _():
            some = slow.at[pl.ds(0, groups - 1), rows, :]
            remote(some, some, slow_send, slow_recv.at[i], (lat, fr)).wait_recv()

        wave_copy(n).wait()
        scale = 2.0 * math.pi * freq_step * freq_ref[m].astype(jnp.float32) * depth_step
        slot = n % 2

        def tile(t, c0):
            r = pl.multiple_of(t * 8, 8)
            at_slow = pl.ds(pl.multiple_of(i * CHUNK + t * 8, 8), 8)
            cells = []
            for k in range(factor):
                at = k * LANES
                s = slow[at // part_width, at_slow, pl.ds(at % part_width, LANES)]
                sn, cs = sin_cos(s * scale)
                re = wave[slot, 0, pl.ds(r, 8), pl.ds(at, LANES)]
                im = wave[slot, 1, pl.ds(r, 8), pl.ds(at, LANES)]
                cells.append((re * cs - im * sn, re * sn + im * cs))
            for k, (re, im) in enumerate(fft_list(cells, -1.0)):
                if k:
                    c, s = tw_ref[0, pl.ds(k, 1), :], tw_ref[1, pl.ds(k, 1), :]
                    re, im = re * c + im * s, im * c - re * s
                zc[k, pl.ds(r, 8), pl.ds(0, LANES)] = re
                zc[k, pl.ds(r, 8), pl.ds(LANES, LANES)] = im
            return c0

        lax.fori_loop(0, CHUNK // 8, tile, 0)
        high, low = split(zc[...].reshape(factor * CHUNK, 2 * LANES))
        y = dot(high, m_fwd[0]) + (dot(low, m_fwd[0]) + dot(high, m_fwd[1]))
        y = y.reshape(factor, CHUNK, 2 * LANES)
        for k in range(factor):
            at = k * LANES
            cols = pl.ds(at % width, LANES)
            spec_out[m, at // width, 0, rows, cols] = y[k, :, :LANES]
            spec_out[m, at // width, 1, rows, cols] = y[k, :, LANES:]
        for mask in lat_masks:
            to = lat_peer(mask)
            remote(
                spec_out.at[m, to, :, rows, :], spec_in.at[m, lat, :, rows, :],
                spec_send.at[m], spec_recv.at[m, lat], (to, fr),
            ).start()
        pltpu.make_async_copy(
            spec_out.at[m, lat, :, rows, :], spec_in.at[m, lat, :, rows, :], spec_own.at[m]
        ).start()

        @pl.when(n == blocks - 1)
        def _():
            def add(t, sums):
                at_slow = pl.ds(pl.multiple_of(t * 8, 8), 8)
                for p in range(groups):
                    for at in range(0, part_width, LANES):
                        sums = sums + slow[p, at_slow, pl.ds(at, LANES)]
                return sums

            total = lax.fori_loop(0, rows_in // 8, add, jnp.zeros((8, LANES), jnp.float32))
            total = jnp.sum(total, axis=0, keepdims=True)
            stat_out[...] = total
            stat_in[lat] = total
            for mask in lat_masks:
                remote(
                    stat_out, stat_in.at[lat], stat_send, stat_recv, (lat_peer(mask), fr)
                ).start()

        return carry

    lax.fori_loop(0, members * blocks, forward, 0)

    source_copy(0).start()
    for copy in late:
        copy.start()
    some = stat_in.at[pl.ds(0, strips - 1)]
    remote(some, some, stat_send, stat_recv, (lat, fr)).wait_recv()
    for copy in late:
        copy.wait()
    mean = jnp.sum(stat_in[...]) * (1.0 / (count * full))

    def shift(m, carry):
        own = spec_in.at[m, lat]
        pltpu.make_async_copy(own, own, spec_own.at[m]).wait()
        for mask in lat_masks:
            peer = lat_peer(mask)
            whole_in = spec_in.at[m, peer]
            remote(whole_in, whole_in, spec_send.at[m], spec_recv.at[m, peer], (lat, fr)).wait_recv()

        def tile_in(t, c0):
            r = pl.multiple_of(t * 8, 8)
            for lane in range(0, width, LANES):
                lanes = pl.ds(lane, LANES)
                cells = []
                for n in range(factor):
                    at = n * LANES
                    rows = pl.ds(at % rows_in + r, 8)
                    cells.append(
                        (spec_in[m, at // rows_in, 0, rows, lanes],
                         spec_in[m, at // rows_in, 1, rows, lanes])
                    )
                for k, (re, im) in enumerate(fft_list(cells, -1.0)):
                    if k:
                        c, s = twx[0, k, pl.ds(r, 8), :], twx[1, k, pl.ds(r, 8), :]
                        re, im = re * c + im * s, im * c - re * s
                    zs[k, pl.ds(r, 8), lanes] = re
                    zs[k, pl.ds(LANES + r, 8), lanes] = im
            return c0

        lax.fori_loop(0, LANES // 8, tile_in, 0)

        angular_mean = 2.0 * math.pi * freq_step * freq_ref[m].astype(jnp.float32) * mean
        flat = angular_mean * depth_step
        place = lat * width + lax.broadcasted_iota(jnp.int32, (LANES, width), 1)
        index_y = place // LANES + factor * (place % LANES)
        signed_y = jnp.where(index_y < full // 2, index_y, index_y - full)
        wave_y = 2.0 * math.pi / (full * grid_step) * signed_y.astype(jnp.float32)
        rest = angular_mean * angular_mean - wave_y * wave_y
        row = lax.broadcasted_iota(jnp.int32, (LANES, width), 0)

        def product(k, c0):
            high, low = split(zs[k])
            y = dot(m_both[0], high) + (dot(m_both[0], low) + dot(m_both[1], high))
            index_x = k + factor * row
            signed_x = jnp.where(index_x < count // 2, index_x, index_x - count)
            wave_x = 2.0 * math.pi / (count * grid_step) * signed_x.astype(jnp.float32)
            vertical = rest - wave_x * wave_x
            size = jnp.sqrt(jnp.abs(vertical)) * depth_step
            damping = jnp.where(vertical < 0.0, jnp.exp(-size), 1.0) * (1.0 / (count * full))
            sn, cs = sin_cos(jnp.where(vertical > 0.0, size, 0.0) - flat)
            tr, ti = damping * cs, damping * sn
            re, im = y[:LANES], y[LANES:]
            z = jnp.concatenate([re * tr - im * ti, re * ti + im * tr], axis=0)
            high, low = split(z)
            zs[k] = dot(m_both[2], high) + (dot(m_both[2], low) + dot(m_both[3], high))
            return c0

        lax.fori_loop(0, factor, product, 0)
        some = spec_out.at[m, pl.ds(0, strips - 1)]
        remote(some, some, spec_send.at[m], spec_recv.at[m, 0], (lat, fr)).wait_send()

        def tile_out(t, c0):
            r = pl.multiple_of(t * 8, 8)
            for lane in range(0, width, LANES):
                lanes = pl.ds(lane, LANES)
                cells = []
                for k in range(factor):
                    re, im = zs[k, pl.ds(r, 8), lanes], zs[k, pl.ds(LANES + r, 8), lanes]
                    if k:
                        c, s = twx[0, k, pl.ds(r, 8), :], twx[1, k, pl.ds(r, 8), :]
                        re, im = re * c - im * s, im * c + re * s
                    cells.append((re, im))
                for n, (re, im) in enumerate(fft_list(cells, 1.0)):
                    at = n * LANES
                    rows = pl.ds(at % rows_in + r, 8)
                    spec_out[m, at // rows_in, 0, rows, lanes] = re
                    spec_out[m, at // rows_in, 1, rows, lanes] = im
            return c0

        lax.fori_loop(0, LANES // 8, tile_out, 0)

        for d in range(strips):
            for c in range(2):
                for e in range(2):
                    beside = d - 1 if e == 0 else d + 1
                    at_row = rows_in - 1 if e == 0 else 0
                    for b in range(lane_blocks):
                        if 0 <= beside < strips:
                            value = spec_out[m, beside, c, pl.ds(at_row, 1), pl.ds(b * LANES, LANES)]
                        else:
                            value = jnp.zeros((1, LANES), jnp.float32)
                        at = (c * 2 + e) * lane_blocks + b
                        edge_out[m, d, pl.ds(at, 1), :] = value

        for mask in lat_masks:
            to = lat_peer(mask)
            remote(
                edge_out.at[m, to], edge_in.at[m, lat], edge_send.at[m], edge_recv.at[m], (to, fr)
            ).start()
        pltpu.make_async_copy(edge_out.at[m, lat], edge_in.at[m, lat], edge_own.at[m]).start()

        def send_lines(i, c0):
            rows = piece_rows(i)
            for mask in lat_masks:
                to = lat_peer(mask)
                remote(
                    spec_out.at[m, to, :, rows, :], line_in.at[m, lat, :, rows, :],
                    line_send.at[m], line_recv.at[m, i], (to, fr),
                ).start()
            pltpu.make_async_copy(
                spec_out.at[m, lat, :, rows, :], line_in.at[m, lat, :, rows, :], line_own.at[m, i]
            ).start()
            return c0

        lax.fori_loop(0, pieces, send_lines, 0)
        return carry

    lax.fori_loop(0, members, shift, 0)

    def columns(z, rows):
        cells = []
        for k in range(factor):
            re, im = z[k, rows, pl.ds(0, LANES)], z[k, rows, pl.ds(LANES, LANES)]
            if k:
                c, s = tw_ref[0, pl.ds(k, 1), :], tw_ref[1, pl.ds(k, 1), :]
                re, im = re * c - im * s, im * c + re * s
            cells.append((re, im))
        return fft_list(cells, 1.0)

    def inverse_dot(x):
        high, low = split(x)
        return dot(high, m_inv[0]) + (dot(low, m_inv[0]) + dot(high, m_inv[1]))

    def edges(m):
        own = edge_in.at[m, lat]
        pltpu.make_async_copy(own, own, edge_own.at[m]).wait()
        some = edge_in.at[m, pl.ds(0, strips - 1)]
        remote(some, some, edge_send.at[m], edge_recv.at[m], (lat, fr)).wait_recv()
        ze[...] = jnp.zeros_like(ze)
        for k in range(factor):
            at = k * LANES
            b = (at % width) // LANES
            for c in range(2):
                for e in range(2):
                    row_at = (c * 2 + e) * lane_blocks + b
                    ze[k, pl.ds(e, 1), pl.ds(c * LANES, LANES)] = edge_in[
                        m, at // width, pl.ds(row_at, 1), :
                    ]
        y = inverse_dot(ze[...].reshape(factor * 8, 2 * LANES))
        ze[...] = y.reshape(factor, 8, 2 * LANES)
        for n, pair in enumerate(columns(ze, pl.ds(0, 8))):
            for c in range(2):
                field[c, pl.ds(7, 1), pl.ds(n * LANES, LANES)] = pair[c][0:1]
                field[c, pl.ds(8 + rows_in, 1), pl.ds(n * LANES, LANES)] = pair[c][1:2]

    def inverse_block(m, i):
        rows = piece_rows(i)
        own = line_in.at[m, lat, :, rows, :]
        pltpu.make_async_copy(own, own, line_own.at[m, i]).wait()
        some = line_in.at[m, pl.ds(0, strips - 1), :, rows, :]
        remote(some, some, line_send.at[m], line_recv.at[m, i], (lat, fr)).wait_recv()
        parts = []
        for k in range(factor):
            at = k * LANES
            cols = pl.ds(at % width, LANES)
            parts.append(
                jnp.concatenate(
                    [line_in[m, at // width, 0, rows, cols], line_in[m, at // width, 1, rows, cols]],
                    axis=1,
                )
            )
        y = inverse_dot(jnp.concatenate(parts, axis=0))
        zp[...] = y.reshape(factor, PIECE, 2 * LANES)

        def tile(t, c0):
            r = pl.multiple_of(t * 8, 8)
            at_field = pl.ds(pl.multiple_of(8 + i * PIECE + t * 8, 8), 8)
            for n, pair in enumerate(columns(zp, pl.ds(r, 8))):
                for c in range(2):
                    field[c, at_field, pl.ds(n * LANES, LANES)] = pair[c]
            return c0

        lax.fori_loop(0, PIECE // 8, tile, 0)

    column = lax.broadcasted_iota(jnp.int32, (PIECE, full), 1)

    def stencil(m, i):
        n = m * pieces + i
        slot = n % 2
        rows = piece_rows(i)

        @pl.when(n + 1 < members * pieces)
        def _():
            source_copy(n + 1).start()

        source_copy(n).wait()
        angular = 2.0 * math.pi * freq_step * freq_ref[m].astype(jnp.float32)
        ahead = 0.5 / (angular * mean)
        start = pl.multiple_of(i * PIECE, PIECE)
        centre, laplace = [], []
        for c in range(2):
            cells = field[c, pl.ds(start, PIECE + 16), :]
            mid = cells[8 : 8 + PIECE]
            up = pltpu.roll(cells, 1, 0)[8 : 8 + PIECE]
            down = pltpu.roll(cells, PIECE + 15, 0)[8 : 8 + PIECE]
            left = jnp.where(column == 0, 0.0, pltpu.roll(mid, 1, 1))
            right = jnp.where(column == full - 1, 0.0, pltpu.roll(mid, full - 1, 1))
            centre.append(mid)
            laplace.append(up + down + left + right - 4.0 * mid)
        slow_rows = jnp.concatenate([slow[p, rows, :] for p in range(groups)], axis=1)
        gain = (ahead - 0.5 / (angular * slow_rows)) * (depth_step / (grid_step * grid_step))
        new_re = centre[0] + gain * laplace[1]
        new_im = centre[1] - gain * laplace[0]
        fresh[0, m, rows, :] = new_re
        fresh[1, m, rows, :] = new_im
        term = (new_re * source[slot, 0] + new_im * source[slot, 1]) * (
            1.0 / math.sqrt(batch_total)
        )
        for p in range(groups):
            part = term[:, p * part_width : (p + 1) * part_width]

            @pl.when(m == 0)
            def _():
                terms[p, rows, :] = part

            @pl.when(m > 0)
            def _():
                terms[p, rows, :] = terms[p, rows, :] + part

        @pl.when(m == members - 1)
        def _():
            for mask in freq_masks:
                to = freq_peer(mask)
                remote(
                    terms.at[to, rows, :], terms_in.at[fr, rows, :], term_send, term_recv,
                    (lat, to),
                ).start()
            terms_in[fr, rows, :] = terms[fr, rows, :]

    def finish(n, carry):
        m, j = n // (pieces + 1), n % (pieces + 1)

        @pl.when(j == 0)
        def _():
            edges(m)

        @pl.when(j < pieces)
        def _():
            inverse_block(m, j)

        @pl.when(j > 0)
        def _():
            stencil(m, j - 1)

        return carry

    lax.fori_loop(0, members * (pieces + 1), finish, 0)
    some = slow.at[pl.ds(0, groups - 1)]
    remote(some, some, slow_send, slow_recv.at[0], (lat, fr)).wait_send()
    some = terms.at[pl.ds(0, groups - 1)]
    remote(some, some, term_send, term_recv, (lat, fr)).wait()
    some = stat_in.at[pl.ds(0, strips - 1)]
    remote(some, some, stat_send, stat_recv, (lat, fr)).wait_send()
    for m in range(members):
        some = spec_out.at[m, pl.ds(0, strips - 1)]
        remote(some, some, line_send.at[m], line_recv.at[m, 0], (lat, fr)).wait_send()
        some = edge_out.at[m, pl.ds(0, strips - 1)]
        remote(some, some, edge_send.at[m], edge_recv.at[m], (lat, fr)).wait_send()


def write_kernel(fresh, terms, field_hbm, image_hbm, image, field_sem, image_sem):
    rows = fresh.shape[2]
    part = rows // 4
    for r in range(0, rows, part):
        for c in range(fresh.shape[0]):
            for m in range(fresh.shape[1]):
                pltpu.make_async_copy(
                    fresh.at[c, m, pl.ds(r, part)], field_hbm.at[c, m, pl.ds(r, part)], field_sem
                ).start()
    total = terms[0]
    for p in range(1, terms.shape[0]):
        total = total + terms[p]
    image[...] = total
    copy = pltpu.make_async_copy(image, image_hbm, image_sem)
    copy.start()
    copy.wait()
    pltpu.make_async_copy(fresh, field_hbm, field_sem).wait()


def local(wavefield, source_field, slowness, freq_index):
    _, members, rows, full = wavefield.shape
    strips, groups = lax.axis_size("lat"), lax.axis_size("freq")
    width = full // strips
    factor = full // LANES
    part_width = full // groups
    blocks, pieces = rows // CHUNK, rows // PIECE
    tw = twiddle(full)
    tw_row = jnp.asarray(tw)
    tw_x = jnp.asarray(np.ascontiguousarray(np.broadcast_to(tw[..., None], tw.shape + (LANES,))))
    right_fwd, right_inv = dft_tables(-1.0), dft_tables(1.0)
    m_fwd, m_inv = split_table(right_fwd), split_table(right_inv)
    m_both = jnp.concatenate(
        [split_table(np.ascontiguousarray(right_fwd.T)), split_table(np.ascontiguousarray(right_inv.T))]
    )
    edge_rows = max(8, 4 * width // LANES)
    far = pl.BlockSpec(memory_space=pltpu.HBM)
    anywhere = pl.BlockSpec(memory_space=pl.ANY)
    inside = pl.BlockSpec(memory_space=pltpu.VMEM)
    f32 = jnp.float32
    dma = pltpu.SemaphoreType.DMA
    fresh, terms = pl.pallas_call(
        functools.partial(step_kernel, batch_total=members * groups),
        in_specs=[pl.BlockSpec(memory_space=pltpu.SMEM)] + [far] * 8,
        out_specs=[inside, inside],
        out_shape=[
            pltpu.VMEM((2, members, rows, full), f32),
            pltpu.VMEM((groups, rows, part_width), f32),
        ],
        scratch_shapes=[
            pltpu.VMEM((members, strips, 2, rows, width), f32),
            pltpu.VMEM((members, strips, 2, rows, width), f32),
            pltpu.VMEM((members, strips, 2, rows, width), f32),
            pltpu.VMEM((members, strips, edge_rows, LANES), f32),
            pltpu.VMEM((members, strips, edge_rows, LANES), f32),
            pltpu.VMEM((1, LANES), f32),
            pltpu.VMEM((strips, 1, LANES), f32),
            pltpu.VMEM((groups, rows, part_width), f32),
            pltpu.VMEM((groups, rows, part_width), f32),
            pltpu.VMEM((factor, 2 * LANES, width), f32),
            pltpu.VMEM((factor, CHUNK, 2 * LANES), f32),
            pltpu.VMEM((factor, PIECE, 2 * LANES), f32),
            pltpu.VMEM((factor, 8, 2 * LANES), f32),
            pltpu.VMEM((2, rows + 16, full), f32),
            pltpu.VMEM((2, 2, CHUNK, full), f32),
            pltpu.VMEM((2, 2, PIECE, full), f32),
            pltpu.VMEM(tw_x.shape, f32),
            pltpu.VMEM(tw_row.shape, f32),
            pltpu.VMEM(m_fwd.shape, m_fwd.dtype),
            pltpu.VMEM(m_both.shape, m_both.dtype),
            pltpu.VMEM(m_inv.shape, m_inv.dtype),
            dma((2,)), dma((2,)), dma((2,)), dma((3,)), dma,
            dma, dma((blocks,)),
            dma((members,)), dma((members, strips)), dma((members,)),
            dma((members,)), dma((members, pieces)), dma((members, pieces)),
            dma((members,)), dma((members,)), dma((members,)),
            dma, dma,
            dma, dma,
        ],
        compiler_params=pltpu.CompilerParams(
            collective_id=0, has_side_effects=True, vmem_limit_bytes=VMEM_BYTES
        ),
        cost_estimate=pl.CostEstimate(
            flops=13_000_000_000, bytes_accessed=26_000_000, transcendentals=0
        ),
        name="depth_step",
    )(freq_index, wavefield, source_field, slowness, tw_x, tw_row, m_fwd, m_both, m_inv)
    return pl.pallas_call(
        write_kernel,
        in_specs=[inside, inside],
        out_specs=[anywhere, anywhere],
        out_shape=[
            jax.ShapeDtypeStruct((2, members, rows, full), f32),
            jax.ShapeDtypeStruct((rows, part_width), f32),
        ],
        scratch_shapes=[pltpu.VMEM((rows, part_width), f32), dma, dma],
        compiler_params=pltpu.CompilerParams(vmem_limit_bytes=SMALL_BYTES),
        cost_estimate=pl.CostEstimate(flops=400_000, bytes_accessed=8_400_000, transcendentals=0),
        name="write_out",
    )(fresh, terms)


def solution(mesh):
    return jax.shard_map(
        local,
        mesh=mesh,
        in_specs=(
            P(None, "freq", "lat", None),
            P(None, "freq", "lat", None),
            P("lat", "freq"),
            P("freq"),
        ),
        out_specs=(P(None, "freq", "lat", None), P("lat", "freq")),
        check_vma=False,
    )
```

```python
import functools
import math

import jax
import jax.numpy as jnp
import numpy as np
from jax import lax
from jax.experimental import pallas as pl
from jax.experimental.pallas import tpu as pltpu
from jax.sharding import PartitionSpec as P

depth_step = 10.0
grid_step = 25.0
freq_step = 0.0625
LANES = 128
CHUNK = 8
PIECE = 8
AHEAD = 2
VMEM_BYTES = 52 * 1024 * 1024
SMALL_BYTES = 4 * 1024 * 1024
MESH = pl.DeviceIdType.MESH


def dft_tables(sign):
    i = np.arange(LANES)
    ang = 2.0 * math.pi / LANES * ((i[:, None] * i[None, :]) % LANES)
    c, s = np.cos(ang), sign * np.sin(ang)
    return np.block([[c, s], [-s, c]])


def split_table(table):
    high = jnp.asarray(table.astype(np.float32)).astype(jnp.bfloat16)
    high64 = np.asarray(table.astype(np.float32).astype(jnp.bfloat16)).astype(np.float64)
    low = (table - high64).astype(np.float32).astype(jnp.bfloat16)
    return jnp.stack([high, jnp.asarray(low)])


def twiddle(count):
    factor = count // LANES
    k, n = np.arange(factor), np.arange(LANES)
    ang = 2.0 * math.pi / count * ((k[:, None] * n[None, :]) % count)
    return np.stack([np.cos(ang), np.sin(ang)]).astype(np.float32)


def fft_list(values, sign):
    count = len(values)
    if count == 1:
        return values
    even, odd = fft_list(values[0::2], sign), fft_list(values[1::2], sign)
    low, high = [], []
    for k in range(count // 2):
        (er, ei), (r, i) = even[k], odd[k]
        if k == 0:
            tr, ti = r, i
        elif 4 * k == count:
            tr, ti = (-i, r) if sign > 0 else (i, -r)
        else:
            c = math.cos(2.0 * math.pi * k / count)
            s = sign * math.sin(2.0 * math.pi * k / count)
            if abs(abs(c) - abs(s)) < 1e-9:
                h = math.sqrt(0.5)
                sc, ss = (1 if c > 0 else -1), (1 if s > 0 else -1)
                tr = h * (r - i) if sc * ss > 0 else h * (r + i)
                ti = h * (i + r) if sc * ss > 0 else h * (i - r)
                if sc < 0:
                    tr, ti = -tr, -ti
            else:
                tr, ti = c * r - s * i, c * i + s * r
        low.append((er + tr, ei + ti))
        high.append((er - tr, ei - ti))
    return low + high


def sin_cos(angle):
    turns = jnp.round(angle * (0.5 / math.pi))
    r = angle - turns * 6.28125 - turns * (2.0 * math.pi - 6.28125)
    r2 = r * r
    s = jnp.full_like(r, 1.0 / math.factorial(17))
    for n in range(15, 0, -2):
        s = s * r2 + ((-1) ** (n // 2)) / math.factorial(n)
    c = jnp.full_like(r, -1.0 / math.factorial(18))
    for n in range(16, -1, -2):
        c = c * r2 + ((-1) ** (n // 2)) / math.factorial(n)
    return s * r, c


def split(x):
    high = x.astype(jnp.bfloat16)
    return high, (x - high.astype(jnp.float32)).astype(jnp.bfloat16)


def dot(a, b):
    return jnp.dot(a, b, preferred_element_type=jnp.float32)


def flipped(index, mask, count):
    other, bit = index, 1
    while bit < count:
        if mask & bit:
            other = other + bit * (1 - 2 * ((index // bit) % 2))
        bit *= 2
    return other


def step_kernel(
    freq_ref, wave_hbm, src_hbm, slow_hbm, twx_hbm, tw_hbm, fwd_hbm, both_hbm, inv_hbm,
    fresh, terms_in,
    spec_out, spec_in, line_in, edge_out, edge_in, stat_out, stat_in,
    slow, terms, zs, zc, zp, ze, field, wave, source,
    twx, tw_ref, m_fwd, m_both, m_inv,
    wave_sem, source_sem, early_sem, late_sem, own_sem,
    slow_send, slow_recv, spec_send, spec_recv, spec_own, line_send, line_recv, line_own,
    edge_send, edge_recv, edge_own, stat_send, stat_recv, term_send, term_recv, greet,
    *, batch_total,
):
    members, strips, rows_in, width = (spec_out.shape[i] for i in (0, 1, 3, 4))
    groups, part_width = slow.shape[0], slow.shape[2]
    full = strips * width
    factor = full // LANES
    count = rows_in * strips
    blocks, pieces = rows_in // CHUNK, rows_in // PIECE
    lane_blocks = width // LANES
    lat, fr = lax.axis_index("lat"), lax.axis_index("freq")
    lat_masks = sorted(range(1, strips), key=lambda m: -m)
    freq_masks = list(range(groups - 1, 0, -1))

    def lat_peer(mask):
        return flipped(lat, mask, strips)

    def freq_peer(mask):
        return flipped(fr, mask, groups)

    def chunk_rows(i):
        return pl.ds(pl.multiple_of(i * CHUNK, CHUNK), CHUNK)

    def piece_rows(i):
        return pl.ds(pl.multiple_of(i * PIECE, PIECE), PIECE)

    def remote(a, b, send, recv, to):
        return pltpu.make_async_remote_copy(
            src_ref=a, dst_ref=b, send_sem=send, recv_sem=recv, device_id=to, device_id_type=MESH
        )

    def wave_copy(n):
        rows = chunk_rows(n % blocks)
        return pltpu.make_async_copy(
            wave_hbm.at[:, n // blocks, rows, :], wave.at[n % 2], wave_sem.at[n % 2]
        )

    def source_copy(n):
        rows = piece_rows(n % pieces)
        return pltpu.make_async_copy(
            src_hbm.at[:, n // pieces, rows, :], source.at[n % 2], source_sem.at[n % 2]
        )

    barrier = pltpu.get_barrier_semaphore()
    for mask in freq_masks:
        pl.semaphore_signal(barrier, inc=1, device_id=(lat, freq_peer(mask)), device_id_type=MESH)
    lat_bits = [bit for bit in lat_masks if bit & (bit - 1) == 0]
    for mask in lat_bits:
        pl.semaphore_signal(barrier, inc=1, device_id=(lat_peer(mask), fr), device_id_type=MESH)

    own_slow = pltpu.make_async_copy(slow_hbm, slow.at[fr], own_sem)
    own_slow.start()
    wave_copy(0).start()
    early = [
        pltpu.make_async_copy(a, b, early_sem.at[i])
        for i, (a, b) in enumerate(((tw_hbm, tw_ref), (fwd_hbm, m_fwd)))
    ]
    late = [
        pltpu.make_async_copy(a, b, late_sem.at[i])
        for i, (a, b) in enumerate(((twx_hbm, twx), (both_hbm, m_both), (inv_hbm, m_inv)))
    ]
    for copy in early:
        copy.start()
    pl.semaphore_wait(barrier, len(freq_masks) + len(lat_bits))

    own_slow.wait()
    spans, first = [], 0
    while first < blocks:
        spans.append((first, min(max(first, 1), blocks - first)))
        first += spans[-1][1]
    for g, (first, size) in enumerate(spans):
        rows = pl.ds(first * CHUNK, size * CHUNK)
        for mask in freq_masks:
            remote(
                slow.at[fr, rows, :], slow.at[fr, rows, :], slow_send, slow_recv.at[g],
                (lat, freq_peer(mask)),
            ).start()
    for stage in range(len(lat_bits) - 1):
        for mask in lat_bits:
            pl.semaphore_signal(
                greet.at[stage], inc=1, device_id=(lat_peer(mask), fr), device_id_type=MESH
            )
        pl.semaphore_wait(greet.at[stage], len(lat_bits))
    for copy in early:
        copy.wait()

    def forward(n, carry):
        m, i = n // blocks, n % blocks
        rows = chunk_rows(i)

        @pl.when(n + 1 < members * blocks)
        def _():
            wave_copy(n + 1).start()

        for g, (first, size) in enumerate(spans):
            @pl.when(n == first)
            def _():
                some = slow.at[pl.ds(0, groups - 1), pl.ds(first * CHUNK, size * CHUNK), :]
                remote(some, some, slow_send, slow_recv.at[g], (lat, fr)).wait_recv()

        wave_copy(n).wait()
        scale = 2.0 * math.pi * freq_step * freq_ref[m].astype(jnp.float32) * depth_step
        slot = n % 2

        def tile(t, c0):
            r = pl.multiple_of(t * 8, 8)
            at_slow = pl.ds(pl.multiple_of(i * CHUNK + t * 8, 8), 8)
            cells = []
            for k in range(factor):
                at = k * LANES
                s = slow[at // part_width, at_slow, pl.ds(at % part_width, LANES)]
                sn, cs = sin_cos(s * scale)
                re = wave[slot, 0, pl.ds(r, 8), pl.ds(at, LANES)]
                im = wave[slot, 1, pl.ds(r, 8), pl.ds(at, LANES)]
                cells.append((re * cs - im * sn, re * sn + im * cs))
            for k, (re, im) in enumerate(fft_list(cells, -1.0)):
                if k:
                    c, s = tw_ref[0, pl.ds(k, 1), :], tw_ref[1, pl.ds(k, 1), :]
                    re, im = re * c + im * s, im * c - re * s
                zc[k, pl.ds(r, 8), pl.ds(0, LANES)] = re
                zc[k, pl.ds(r, 8), pl.ds(LANES, LANES)] = im
            return c0

        lax.fori_loop(0, CHUNK // 8, tile, 0)
        high, low = split(zc[...].reshape(factor * CHUNK, 2 * LANES))
        y = dot(high, m_fwd[0]) + (dot(low, m_fwd[0]) + dot(high, m_fwd[1]))
        y = y.reshape(factor, CHUNK, 2 * LANES)
        for k in range(factor):
            at = k * LANES
            cols = pl.ds(at % width, LANES)
            spec_out[m, at // width, 0, rows, cols] = y[k, :, :LANES]
            spec_out[m, at // width, 1, rows, cols] = y[k, :, LANES:]
        for mask in lat_masks:
            to = lat_peer(mask)
            remote(
                spec_out.at[m, to, :, rows, :], spec_in.at[m, lat, :, rows, :],
                spec_send.at[m], spec_recv.at[m, lat], (to, fr),
            ).start()
        pltpu.make_async_copy(
            spec_out.at[m, lat, :, rows, :], spec_in.at[m, lat, :, rows, :], spec_own.at[m]
        ).start()

        @pl.when(n == blocks - 1)
        def _():
            def add(t, sums):
                at_slow = pl.ds(pl.multiple_of(t * 8, 8), 8)
                for p in range(groups):
                    for at in range(0, part_width, LANES):
                        sums = sums + slow[p, at_slow, pl.ds(at, LANES)]
                return sums

            total = lax.fori_loop(0, rows_in // 8, add, jnp.zeros((8, LANES), jnp.float32))
            total = jnp.sum(total, axis=0, keepdims=True)
            stat_out[...] = total
            stat_in[lat] = total
            for mask in lat_masks:
                remote(
                    stat_out, stat_in.at[lat], stat_send, stat_recv, (lat_peer(mask), fr)
                ).start()

        return carry

    lax.fori_loop(0, members * blocks, forward, 0)

    source_copy(0).start()
    for copy in late:
        copy.start()
    some = stat_in.at[pl.ds(0, strips - 1)]
    remote(some, some, stat_send, stat_recv, (lat, fr)).wait_recv()
    for copy in late:
        copy.wait()
    mean = jnp.sum(stat_in[...]) * (1.0 / (count * full))

    def shift(m, carry):
        own = spec_in.at[m, lat]
        pltpu.make_async_copy(own, own, spec_own.at[m]).wait()
        for mask in lat_masks:
            peer = lat_peer(mask)
            whole_in = spec_in.at[m, peer]
            remote(whole_in, whole_in, spec_send.at[m], spec_recv.at[m, peer], (lat, fr)).wait_recv()

        def tile_in(t, c0):
            r = pl.multiple_of(t * 8, 8)
            for lane in range(0, width, LANES):
                lanes = pl.ds(lane, LANES)
                cells = []
                for n in range(factor):
                    at = n * LANES
                    rows = pl.ds(at % rows_in + r, 8)
                    cells.append(
                        (spec_in[m, at // rows_in, 0, rows, lanes],
                         spec_in[m, at // rows_in, 1, rows, lanes])
                    )
                for k, (re, im) in enumerate(fft_list(cells, -1.0)):
                    if k:
                        c, s = twx[0, k, pl.ds(r, 8), :], twx[1, k, pl.ds(r, 8), :]
                        re, im = re * c + im * s, im * c - re * s
                    zs[k, pl.ds(r, 8), lanes] = re
                    zs[k, pl.ds(LANES + r, 8), lanes] = im
            return c0

        lax.fori_loop(0, LANES // 8, tile_in, 0)

        angular_mean = 2.0 * math.pi * freq_step * freq_ref[m].astype(jnp.float32) * mean
        flat = angular_mean * depth_step
        place = lat * width + lax.broadcasted_iota(jnp.int32, (LANES, width), 1)
        index_y = place // LANES + factor * (place % LANES)
        signed_y = jnp.where(index_y < full // 2, index_y, index_y - full)
        wave_y = 2.0 * math.pi / (full * grid_step) * signed_y.astype(jnp.float32)
        rest = angular_mean * angular_mean - wave_y * wave_y
        row = lax.broadcasted_iota(jnp.int32, (LANES, width), 0)

        def product(k, c0):
            high, low = split(zs[k])
            y = dot(m_both[0], high) + (dot(m_both[0], low) + dot(m_both[1], high))
            index_x = k + factor * row
            signed_x = jnp.where(index_x < count // 2, index_x, index_x - count)
            wave_x = 2.0 * math.pi / (count * grid_step) * signed_x.astype(jnp.float32)
            vertical = rest - wave_x * wave_x
            size = jnp.sqrt(jnp.abs(vertical)) * depth_step
            damping = jnp.where(vertical < 0.0, jnp.exp(-size), 1.0) * (1.0 / (count * full))
            sn, cs = sin_cos(jnp.where(vertical > 0.0, size, 0.0) - flat)
            tr, ti = damping * cs, damping * sn
            re, im = y[:LANES], y[LANES:]
            z = jnp.concatenate([re * tr - im * ti, re * ti + im * tr], axis=0)
            high, low = split(z)
            zs[k] = dot(m_both[2], high) + (dot(m_both[2], low) + dot(m_both[3], high))
            return c0

        lax.fori_loop(0, factor, product, 0)
        some = spec_out.at[m, pl.ds(0, strips - 1)]
        remote(some, some, spec_send.at[m], spec_recv.at[m, 0], (lat, fr)).wait_send()

        def tile_out(t, c0):
            r = pl.multiple_of(t * 8, 8)
            for lane in range(0, width, LANES):
                lanes = pl.ds(lane, LANES)
                cells = []
                for k in range(factor):
                    re, im = zs[k, pl.ds(r, 8), lanes], zs[k, pl.ds(LANES + r, 8), lanes]
                    if k:
                        c, s = twx[0, k, pl.ds(r, 8), :], twx[1, k, pl.ds(r, 8), :]
                        re, im = re * c - im * s, im * c + re * s
                    cells.append((re, im))
                for n, (re, im) in enumerate(fft_list(cells, 1.0)):
                    at = n * LANES
                    rows = pl.ds(at % rows_in + r, 8)
                    spec_out[m, at // rows_in, 0, rows, lanes] = re
                    spec_out[m, at // rows_in, 1, rows, lanes] = im
            return c0

        lax.fori_loop(0, LANES // 8, tile_out, 0)

        for d in range(strips):
            for c in range(2):
                for e in range(2):
                    beside = d - 1 if e == 0 else d + 1
                    at_row = rows_in - 1 if e == 0 else 0
                    for b in range(lane_blocks):
                        if 0 <= beside < strips:
                            value = spec_out[m, beside, c, pl.ds(at_row, 1), pl.ds(b * LANES, LANES)]
                        else:
                            value = jnp.zeros((1, LANES), jnp.float32)
                        at = (c * 2 + e) * lane_blocks + b
                        edge_out[m, d, pl.ds(at, 1), :] = value

        for mask in lat_masks:
            to = lat_peer(mask)
            remote(
                edge_out.at[m, to], edge_in.at[m, lat], edge_send.at[m], edge_recv.at[m], (to, fr)
            ).start()
        pltpu.make_async_copy(edge_out.at[m, lat], edge_in.at[m, lat], edge_own.at[m]).start()

        def send_lines(i, c0):
            rows = piece_rows(i)
            for mask in lat_masks:
                to = lat_peer(mask)
                remote(
                    spec_out.at[m, to, :, rows, :], line_in.at[m, lat, :, rows, :],
                    line_send.at[m], line_recv.at[m, i], (to, fr),
                ).start()
            pltpu.make_async_copy(
                spec_out.at[m, lat, :, rows, :], line_in.at[m, lat, :, rows, :], line_own.at[m, i]
            ).start()
            return c0

        lax.fori_loop(0, pieces, send_lines, 0)
        return carry

    lax.fori_loop(0, members, shift, 0)

    def columns(z, rows):
        cells = []
        for k in range(factor):
            re, im = z[k, rows, pl.ds(0, LANES)], z[k, rows, pl.ds(LANES, LANES)]
            if k:
                c, s = tw_ref[0, pl.ds(k, 1), :], tw_ref[1, pl.ds(k, 1), :]
                re, im = re * c - im * s, im * c + re * s
            cells.append((re, im))
        return fft_list(cells, 1.0)

    def inverse_dot(x):
        high, low = split(x)
        return dot(high, m_inv[0]) + (dot(low, m_inv[0]) + dot(high, m_inv[1]))

    def edges(m):
        own = edge_in.at[m, lat]
        pltpu.make_async_copy(own, own, edge_own.at[m]).wait()
        some = edge_in.at[m, pl.ds(0, strips - 1)]
        remote(some, some, edge_send.at[m], edge_recv.at[m], (lat, fr)).wait_recv()
        ze[...] = jnp.zeros_like(ze)
        for k in range(factor):
            at = k * LANES
            b = (at % width) // LANES
            for c in range(2):
                for e in range(2):
                    row_at = (c * 2 + e) * lane_blocks + b
                    ze[k, pl.ds(e, 1), pl.ds(c * LANES, LANES)] = edge_in[
                        m, at // width, pl.ds(row_at, 1), :
                    ]
        y = inverse_dot(ze[...].reshape(factor * 8, 2 * LANES))
        ze[...] = y.reshape(factor, 8, 2 * LANES)
        for n, pair in enumerate(columns(ze, pl.ds(0, 8))):
            for c in range(2):
                field[c, pl.ds(7, 1), pl.ds(n * LANES, LANES)] = pair[c][0:1]
                field[c, pl.ds(8 + rows_in, 1), pl.ds(n * LANES, LANES)] = pair[c][1:2]

    def inverse_block(m, i):
        rows = piece_rows(i)
        own = line_in.at[m, lat, :, rows, :]
        pltpu.make_async_copy(own, own, line_own.at[m, i]).wait()
        some = line_in.at[m, pl.ds(0, strips - 1), :, rows, :]
        remote(some, some, line_send.at[m], line_recv.at[m, i], (lat, fr)).wait_recv()
        parts = []
        for k in range(factor):
            at = k * LANES
            cols = pl.ds(at % width, LANES)
            parts.append(
                jnp.concatenate(
                    [line_in[m, at // width, 0, rows, cols], line_in[m, at // width, 1, rows, cols]],
                    axis=1,
                )
            )
        y = inverse_dot(jnp.concatenate(parts, axis=0))
        zp[...] = y.reshape(factor, PIECE, 2 * LANES)

        def tile(t, c0):
            r = pl.multiple_of(t * 8, 8)
            at_field = pl.ds(pl.multiple_of(8 + i * PIECE + t * 8, 8), 8)
            for n, pair in enumerate(columns(zp, pl.ds(r, 8))):
                for c in range(2):
                    field[c, at_field, pl.ds(n * LANES, LANES)] = pair[c]
            return c0

        lax.fori_loop(0, PIECE // 8, tile, 0)

    column = lax.broadcasted_iota(jnp.int32, (PIECE, full), 1)

    def stencil(m, i):
        n = m * pieces + i
        slot = n % 2
        rows = piece_rows(i)

        @pl.when(n + 1 < members * pieces)
        def _():
            source_copy(n + 1).start()

        source_copy(n).wait()
        angular = 2.0 * math.pi * freq_step * freq_ref[m].astype(jnp.float32)
        ahead = 0.5 / (angular * mean)
        start = pl.multiple_of(i * PIECE, PIECE)
        centre, laplace = [], []
        for c in range(2):
            cells = field[c, pl.ds(start, PIECE + 16), :]
            mid = cells[8 : 8 + PIECE]
            up = pltpu.roll(cells, 1, 0)[8 : 8 + PIECE]
            down = pltpu.roll(cells, PIECE + 15, 0)[8 : 8 + PIECE]
            left = jnp.where(column == 0, 0.0, pltpu.roll(mid, 1, 1))
            right = jnp.where(column == full - 1, 0.0, pltpu.roll(mid, full - 1, 1))
            centre.append(mid)
            laplace.append(up + down + left + right - 4.0 * mid)
        slow_rows = jnp.concatenate([slow[p, rows, :] for p in range(groups)], axis=1)
        gain = (ahead - 0.5 / (angular * slow_rows)) * (depth_step / (grid_step * grid_step))
        new_re = centre[0] + gain * laplace[1]
        new_im = centre[1] - gain * laplace[0]
        fresh[0, m, rows, :] = new_re
        fresh[1, m, rows, :] = new_im
        term = (new_re * source[slot, 0] + new_im * source[slot, 1]) * (
            1.0 / math.sqrt(batch_total)
        )
        for p in range(groups):
            part = term[:, p * part_width : (p + 1) * part_width]

            @pl.when(m == 0)
            def _():
                terms[p, rows, :] = part

            @pl.when(m > 0)
            def _():
                terms[p, rows, :] = terms[p, rows, :] + part

        @pl.when(m == members - 1)
        def _():
            for mask in freq_masks:
                to = freq_peer(mask)
                remote(
                    terms.at[to, rows, :], terms_in.at[fr, rows, :], term_send, term_recv,
                    (lat, to),
                ).start()
            terms_in[fr, rows, :] = terms[fr, rows, :]

    def finish(n, carry):
        m, j = n // (pieces + 1), n % (pieces + 1)

        @pl.when(j == 0)
        def _():
            edges(m)

        @pl.when(j < pieces)
        def _():
            inverse_block(m, j)

        @pl.when(j > 0)
        def _():
            stencil(m, j - 1)

        return carry

    lax.fori_loop(0, members * (pieces + 1), finish, 0)
    some = slow.at[pl.ds(0, groups - 1)]
    remote(some, some, slow_send, slow_recv.at[0], (lat, fr)).wait_send()
    some = terms.at[pl.ds(0, groups - 1)]
    remote(some, some, term_send, term_recv, (lat, fr)).wait()
    some = stat_in.at[pl.ds(0, strips - 1)]
    remote(some, some, stat_send, stat_recv, (lat, fr)).wait_send()
    for m in range(members):
        some = spec_out.at[m, pl.ds(0, strips - 1)]
        remote(some, some, line_send.at[m], line_recv.at[m, 0], (lat, fr)).wait_send()
        some = edge_out.at[m, pl.ds(0, strips - 1)]
        remote(some, some, edge_send.at[m], edge_recv.at[m], (lat, fr)).wait_send()


def write_kernel(fresh, terms, field_hbm, image_hbm, image, field_sem, image_sem):
    rows = fresh.shape[2]
    part = rows // 16
    for r in range(0, rows, part):
        for c in range(fresh.shape[0]):
            for m in range(fresh.shape[1]):
                pltpu.make_async_copy(
                    fresh.at[c, m, pl.ds(r, part)], field_hbm.at[c, m, pl.ds(r, part)], field_sem
                ).start()
    total = terms[0]
    for p in range(1, terms.shape[0]):
        total = total + terms[p]
    image[...] = total
    copy = pltpu.make_async_copy(image, image_hbm, image_sem)
    copy.start()
    copy.wait()
    pltpu.make_async_copy(fresh, field_hbm, field_sem).wait()


def local(wavefield, source_field, slowness, freq_index):
    _, members, rows, full = wavefield.shape
    strips, groups = lax.axis_size("lat"), lax.axis_size("freq")
    width = full // strips
    factor = full // LANES
    part_width = full // groups
    blocks, pieces = rows // CHUNK, rows // PIECE
    tw = twiddle(full)
    tw_row = jnp.asarray(tw)
    tw_x = jnp.asarray(np.ascontiguousarray(np.broadcast_to(tw[..., None], tw.shape + (LANES,))))
    right_fwd, right_inv = dft_tables(-1.0), dft_tables(1.0)
    m_fwd, m_inv = split_table(right_fwd), split_table(right_inv)
    m_both = jnp.concatenate(
        [split_table(np.ascontiguousarray(right_fwd.T)), split_table(np.ascontiguousarray(right_inv.T))]
    )
    edge_rows = max(8, 4 * width // LANES)
    far = pl.BlockSpec(memory_space=pltpu.HBM)
    anywhere = pl.BlockSpec(memory_space=pl.ANY)
    inside = pl.BlockSpec(memory_space=pltpu.VMEM)
    f32 = jnp.float32
    dma = pltpu.SemaphoreType.DMA
    fresh, terms = pl.pallas_call(
        functools.partial(step_kernel, batch_total=members * groups),
        in_specs=[pl.BlockSpec(memory_space=pltpu.SMEM)] + [far] * 8,
        out_specs=[inside, inside],
        out_shape=[
            pltpu.VMEM((2, members, rows, full), f32),
            pltpu.VMEM((groups, rows, part_width), f32),
        ],
        scratch_shapes=[
            pltpu.VMEM((members, strips, 2, rows, width), f32),
            pltpu.VMEM((members, strips, 2, rows, width), f32),
            pltpu.VMEM((members, strips, 2, rows, width), f32),
            pltpu.VMEM((members, strips, edge_rows, LANES), f32),
            pltpu.VMEM((members, strips, edge_rows, LANES), f32),
            pltpu.VMEM((1, LANES), f32),
            pltpu.VMEM((strips, 1, LANES), f32),
            pltpu.VMEM((groups, rows, part_width), f32),
            pltpu.VMEM((groups, rows, part_width), f32),
            pltpu.VMEM((factor, 2 * LANES, width), f32),
            pltpu.VMEM((factor, CHUNK, 2 * LANES), f32),
            pltpu.VMEM((factor, PIECE, 2 * LANES), f32),
            pltpu.VMEM((factor, 8, 2 * LANES), f32),
            pltpu.VMEM((2, rows + 16, full), f32),
            pltpu.VMEM((2, 2, CHUNK, full), f32),
            pltpu.VMEM((2, 2, PIECE, full), f32),
            pltpu.VMEM(tw_x.shape, f32),
            pltpu.VMEM(tw_row.shape, f32),
            pltpu.VMEM(m_fwd.shape, m_fwd.dtype),
            pltpu.VMEM(m_both.shape, m_both.dtype),
            pltpu.VMEM(m_inv.shape, m_inv.dtype),
            dma((2,)), dma((2,)), dma((2,)), dma((3,)), dma,
            dma, dma((blocks,)),
            dma((members,)), dma((members, strips)), dma((members,)),
            dma((members,)), dma((members, pieces)), dma((members, pieces)),
            dma((members,)), dma((members,)), dma((members,)),
            dma, dma,
            dma, dma,
            pltpu.SemaphoreType.REGULAR((max(strips.bit_length() - 2, 1),)),
        ],
        compiler_params=pltpu.CompilerParams(
            collective_id=0, has_side_effects=True, vmem_limit_bytes=VMEM_BYTES
        ),
        cost_estimate=pl.CostEstimate(
            flops=13_000_000_000, bytes_accessed=26_000_000, transcendentals=0
        ),
        name="depth_step",
    )(freq_index, wavefield, source_field, slowness, tw_x, tw_row, m_fwd, m_both, m_inv)
    return pl.pallas_call(
        write_kernel,
        in_specs=[inside, inside],
        out_specs=[anywhere, anywhere],
        out_shape=[
            jax.ShapeDtypeStruct((2, members, rows, full), f32),
            jax.ShapeDtypeStruct((rows, part_width), f32),
        ],
        scratch_shapes=[pltpu.VMEM((rows, part_width), f32), dma, dma],
        compiler_params=pltpu.CompilerParams(vmem_limit_bytes=SMALL_BYTES),
        cost_estimate=pl.CostEstimate(flops=400_000, bytes_accessed=8_400_000, transcendentals=0),
        name="write_out",
    )(fresh, terms)


def solution(mesh):
    return jax.shard_map(
        local,
        mesh=mesh,
        in_specs=(
            P(None, "freq", "lat", None),
            P(None, "freq", "lat", None),
            P("lat", "freq"),
            P("freq"),
        ),
        out_specs=(P(None, "freq", "lat", None), P("lat", "freq")),
        check_vma=False,
    )
```

```python
import functools
import math

import jax
import jax.numpy as jnp
import numpy as np
from jax import lax
from jax.experimental import pallas as pl
from jax.experimental.pallas import tpu as pltpu
from jax.sharding import PartitionSpec as P

depth_step = 10.0
grid_step = 25.0
freq_step = 0.0625
LANES = 128
CHUNK = 8
PIECE = 8
AHEAD = 2
VMEM_BYTES = 52 * 1024 * 1024
SMALL_BYTES = 4 * 1024 * 1024
MESH = pl.DeviceIdType.MESH


def dft_tables(sign):
    i = np.arange(LANES)
    ang = 2.0 * math.pi / LANES * ((i[:, None] * i[None, :]) % LANES)
    c, s = np.cos(ang), sign * np.sin(ang)
    return np.block([[c, s], [-s, c]])


def split_table(table):
    high = jnp.asarray(table.astype(np.float32)).astype(jnp.bfloat16)
    high64 = np.asarray(table.astype(np.float32).astype(jnp.bfloat16)).astype(np.float64)
    low = (table - high64).astype(np.float32).astype(jnp.bfloat16)
    return jnp.stack([high, jnp.asarray(low)])


def twiddle(count):
    factor = count // LANES
    k, n = np.arange(factor), np.arange(LANES)
    ang = 2.0 * math.pi / count * ((k[:, None] * n[None, :]) % count)
    return np.stack([np.cos(ang), np.sin(ang)]).astype(np.float32)


def fft_list(values, sign):
    count = len(values)
    if count == 1:
        return values
    even, odd = fft_list(values[0::2], sign), fft_list(values[1::2], sign)
    low, high = [], []
    for k in range(count // 2):
        (er, ei), (r, i) = even[k], odd[k]
        if k == 0:
            tr, ti = r, i
        elif 4 * k == count:
            tr, ti = (-i, r) if sign > 0 else (i, -r)
        else:
            c = math.cos(2.0 * math.pi * k / count)
            s = sign * math.sin(2.0 * math.pi * k / count)
            if abs(abs(c) - abs(s)) < 1e-9:
                h = math.sqrt(0.5)
                sc, ss = (1 if c > 0 else -1), (1 if s > 0 else -1)
                tr = h * (r - i) if sc * ss > 0 else h * (r + i)
                ti = h * (i + r) if sc * ss > 0 else h * (i - r)
                if sc < 0:
                    tr, ti = -tr, -ti
            else:
                tr, ti = c * r - s * i, c * i + s * r
        low.append((er + tr, ei + ti))
        high.append((er - tr, ei - ti))
    return low + high


def sin_cos(angle):
    turns = jnp.round(angle * (0.5 / math.pi))
    r = angle - turns * 6.28125 - turns * (2.0 * math.pi - 6.28125)
    r2 = r * r
    s = jnp.full_like(r, 1.0 / math.factorial(17))
    for n in range(15, 0, -2):
        s = s * r2 + ((-1) ** (n // 2)) / math.factorial(n)
    c = jnp.full_like(r, -1.0 / math.factorial(18))
    for n in range(16, -1, -2):
        c = c * r2 + ((-1) ** (n // 2)) / math.factorial(n)
    return s * r, c


def split(x):
    high = x.astype(jnp.bfloat16)
    return high, (x - high.astype(jnp.float32)).astype(jnp.bfloat16)


def dot(a, b):
    return jnp.dot(a, b, preferred_element_type=jnp.float32)


def flipped(index, mask, count):
    other, bit = index, 1
    while bit < count:
        if mask & bit:
            other = other + bit * (1 - 2 * ((index // bit) % 2))
        bit *= 2
    return other


def step_kernel(
    freq_hbm, wave_hbm, src_hbm, slow_hbm, twx_hbm, tw_hbm, fwd_hbm, both_hbm, inv_hbm,
    fresh, terms_in,
    spec_out, spec_in, line_in, edge_out, edge_in, stat_out, stat_in,
    slow, terms, zs, zc, zp, ze, field, wave, source,
    twx, tw_ref, m_fwd, m_both, m_inv, freq_ref,
    wave_sem, source_sem, early_sem, late_sem, own_sem,
    slow_send, slow_recv, spec_send, spec_recv, spec_own, line_send, line_recv, line_own,
    edge_send, edge_recv, edge_own, stat_send, stat_recv, term_send, term_recv,
    *, batch_total,
):
    members, strips, rows_in, width = (spec_out.shape[i] for i in (0, 1, 3, 4))
    groups, part_width = slow.shape[0], slow.shape[2]
    full = strips * width
    factor = full // LANES
    count = rows_in * strips
    blocks, pieces = rows_in // CHUNK, rows_in // PIECE
    lane_blocks = width // LANES
    lat, fr = lax.axis_index("lat"), lax.axis_index("freq")
    lat_masks = sorted(range(1, strips), key=lambda m: -m)
    freq_masks = list(range(1, groups))

    def lat_peer(mask):
        return flipped(lat, mask, strips)

    def freq_peer(mask):
        return flipped(fr, mask, groups)

    def chunk_rows(i):
        return pl.ds(pl.multiple_of(i * CHUNK, CHUNK), CHUNK)

    def piece_rows(i):
        return pl.ds(pl.multiple_of(i * PIECE, PIECE), PIECE)

    def remote(a, b, send, recv, to):
        return pltpu.make_async_remote_copy(
            src_ref=a, dst_ref=b, send_sem=send, recv_sem=recv, device_id=to, device_id_type=MESH
        )

    def wave_copy(n):
        rows = chunk_rows(n % blocks)
        return pltpu.make_async_copy(
            wave_hbm.at[:, n // blocks, rows, :], wave.at[n % 2], wave_sem.at[n % 2]
        )

    def source_copy(n):
        rows = piece_rows(n % pieces)
        return pltpu.make_async_copy(
            src_hbm.at[:, n // pieces, rows, :], source.at[n % 2], source_sem.at[n % 2]
        )

    barrier = pltpu.get_barrier_semaphore()
    for mask in freq_masks:
        pl.semaphore_signal(barrier, inc=1, device_id=(lat, freq_peer(mask)), device_id_type=MESH)
    for mask in lat_masks:
        pl.semaphore_signal(barrier, inc=1, device_id=(lat_peer(mask), fr), device_id_type=MESH)

    own_slow = pltpu.make_async_copy(slow_hbm, slow.at[fr], own_sem)
    own_slow.start()
    wave_copy(0).start()
    early = [
        pltpu.make_async_copy(a, b, early_sem.at[i])
        for i, (a, b) in enumerate(((tw_hbm, tw_ref), (fwd_hbm, m_fwd), (freq_hbm, freq_ref)))
    ]
    late = [
        pltpu.make_async_copy(a, b, late_sem.at[i])
        for i, (a, b) in enumerate(((twx_hbm, twx), (both_hbm, m_both), (inv_hbm, m_inv)))
    ]
    for copy in early:
        copy.start()
    pl.semaphore_wait(barrier, len(freq_masks) + len(lat_masks))

    def send_slow(i, carry):
        rows = chunk_rows(i)
        for mask in freq_masks:
            remote(
                slow.at[fr, rows, :], slow.at[fr, rows, :], slow_send, slow_recv.at[i],
                (lat, freq_peer(mask)),
            ).start()
        return carry

    own_slow.wait()
    lax.fori_loop(0, min(AHEAD, blocks), send_slow, 0)
    for copy in early:
        copy.wait()

    def forward(n, carry):
        m, i = n // blocks, n % blocks
        rows = chunk_rows(i)

        @pl.when(n + 1 < members * blocks)
        def _():
            wave_copy(n + 1).start()

        @pl.when(n + AHEAD < blocks)
        def _():
            send_slow(n + AHEAD, 0)

        @pl.when(n < blocks)
        def _():
            some = slow.at[pl.ds(0, groups - 1), rows, :]
            remote(some, some, slow_send, slow_recv.at[i], (lat, fr)).wait_recv()

        wave_copy(n).wait()
        scale = 2.0 * math.pi * freq_step * freq_ref[m].astype(jnp.float32) * depth_step
        slot = n % 2

        def tile(t, c0):
            r = pl.multiple_of(t * 8, 8)
            at_slow = pl.ds(pl.multiple_of(i * CHUNK + t * 8, 8), 8)
            cells = []
            for k in range(factor):
                at = k * LANES
                s = slow[at // part_width, at_slow, pl.ds(at % part_width, LANES)]
                sn, cs = sin_cos(s * scale)
                re = wave[slot, 0, pl.ds(r, 8), pl.ds(at, LANES)]
                im = wave[slot, 1, pl.ds(r, 8), pl.ds(at, LANES)]
                cells.append((re * cs - im * sn, re * sn + im * cs))
            for k, (re, im) in enumerate(fft_list(cells, -1.0)):
                if k:
                    c, s = tw_ref[0, pl.ds(k, 1), :], tw_ref[1, pl.ds(k, 1), :]
                    re, im = re * c + im * s, im * c - re * s
                zc[k, pl.ds(r, 8), pl.ds(0, LANES)] = re
                zc[k, pl.ds(r, 8), pl.ds(LANES, LANES)] = im
            return c0

        lax.fori_loop(0, CHUNK // 8, tile, 0)
        high, low = split(zc[...].reshape(factor * CHUNK, 2 * LANES))
        y = dot(high, m_fwd[0]) + (dot(low, m_fwd[0]) + dot(high, m_fwd[1]))
        y = y.reshape(factor, CHUNK, 2 * LANES)
        for k in range(factor):
            at = k * LANES
            cols = pl.ds(at % width, LANES)
            spec_out[m, at // width, 0, rows, cols] = y[k, :, :LANES]
            spec_out[m, at // width, 1, rows, cols] = y[k, :, LANES:]
        for mask in lat_masks:
            to = lat_peer(mask)
            remote(
                spec_out.at[m, to, :, rows, :], spec_in.at[m, lat, :, rows, :],
                spec_send.at[m], spec_recv.at[m, lat], (to, fr),
            ).start()
        pltpu.make_async_copy(
            spec_out.at[m, lat, :, rows, :], spec_in.at[m, lat, :, rows, :], spec_own.at[m]
        ).start()

        @pl.when(n == blocks - 1)
        def _():
            def add(t, sums):
                at_slow = pl.ds(pl.multiple_of(t * 8, 8), 8)
                for p in range(groups):
                    for at in range(0, part_width, LANES):
                        sums = sums + slow[p, at_slow, pl.ds(at, LANES)]
                return sums

            total = lax.fori_loop(0, rows_in // 8, add, jnp.zeros((8, LANES), jnp.float32))
            total = jnp.sum(total, axis=0, keepdims=True)
            stat_out[...] = total
            stat_in[lat] = total
            for mask in lat_masks:
                remote(
                    stat_out, stat_in.at[lat], stat_send, stat_recv, (lat_peer(mask), fr)
                ).start()

        return carry

    lax.fori_loop(0, members * blocks, forward, 0)

    source_copy(0).start()
    for copy in late:
        copy.start()
    some = stat_in.at[pl.ds(0, strips - 1)]
    remote(some, some, stat_send, stat_recv, (lat, fr)).wait_recv()
    for copy in late:
        copy.wait()
    mean = jnp.sum(stat_in[...]) * (1.0 / (count * full))

    def shift(m, carry):
        own = spec_in.at[m, lat]
        pltpu.make_async_copy(own, own, spec_own.at[m]).wait()
        for mask in lat_masks:
            peer = lat_peer(mask)
            whole_in = spec_in.at[m, peer]
            remote(whole_in, whole_in, spec_send.at[m], spec_recv.at[m, peer], (lat, fr)).wait_recv()

        def tile_in(t, c0):
            r = pl.multiple_of(t * 8, 8)
            for lane in range(0, width, LANES):
                lanes = pl.ds(lane, LANES)
                cells = []
                for n in range(factor):
                    at = n * LANES
                    rows = pl.ds(at % rows_in + r, 8)
                    cells.append(
                        (spec_in[m, at // rows_in, 0, rows, lanes],
                         spec_in[m, at // rows_in, 1, rows, lanes])
                    )
                for k, (re, im) in enumerate(fft_list(cells, -1.0)):
                    if k:
                        c, s = twx[0, k, pl.ds(r, 8), :], twx[1, k, pl.ds(r, 8), :]
                        re, im = re * c + im * s, im * c - re * s
                    zs[k, pl.ds(r, 8), lanes] = re
                    zs[k, pl.ds(LANES + r, 8), lanes] = im
            return c0

        lax.fori_loop(0, LANES // 8, tile_in, 0)

        angular_mean = 2.0 * math.pi * freq_step * freq_ref[m].astype(jnp.float32) * mean
        flat = angular_mean * depth_step
        place = lat * width + lax.broadcasted_iota(jnp.int32, (LANES, width), 1)
        index_y = place // LANES + factor * (place % LANES)
        signed_y = jnp.where(index_y < full // 2, index_y, index_y - full)
        wave_y = 2.0 * math.pi / (full * grid_step) * signed_y.astype(jnp.float32)
        rest = angular_mean * angular_mean - wave_y * wave_y
        row = lax.broadcasted_iota(jnp.int32, (LANES, width), 0)

        def product(k, c0):
            high, low = split(zs[k])
            y = dot(m_both[0], high) + (dot(m_both[0], low) + dot(m_both[1], high))
            index_x = k + factor * row
            signed_x = jnp.where(index_x < count // 2, index_x, index_x - count)
            wave_x = 2.0 * math.pi / (count * grid_step) * signed_x.astype(jnp.float32)
            vertical = rest - wave_x * wave_x
            size = jnp.sqrt(jnp.abs(vertical)) * depth_step
            damping = jnp.where(vertical < 0.0, jnp.exp(-size), 1.0) * (1.0 / (count * full))
            sn, cs = sin_cos(jnp.where(vertical > 0.0, size, 0.0) - flat)
            tr, ti = damping * cs, damping * sn
            re, im = y[:LANES], y[LANES:]
            z = jnp.concatenate([re * tr - im * ti, re * ti + im * tr], axis=0)
            high, low = split(z)
            zs[k] = dot(m_both[2], high) + (dot(m_both[2], low) + dot(m_both[3], high))
            return c0

        lax.fori_loop(0, factor, product, 0)
        some = spec_out.at[m, pl.ds(0, strips - 1)]
        remote(some, some, spec_send.at[m], spec_recv.at[m, 0], (lat, fr)).wait_send()

        def tile_out(t, c0):
            r = pl.multiple_of(t * 8, 8)
            for lane in range(0, width, LANES):
                lanes = pl.ds(lane, LANES)
                cells = []
                for k in range(factor):
                    re, im = zs[k, pl.ds(r, 8), lanes], zs[k, pl.ds(LANES + r, 8), lanes]
                    if k:
                        c, s = twx[0, k, pl.ds(r, 8), :], twx[1, k, pl.ds(r, 8), :]
                        re, im = re * c - im * s, im * c + re * s
                    cells.append((re, im))
                for n, (re, im) in enumerate(fft_list(cells, 1.0)):
                    at = n * LANES
                    rows = pl.ds(at % rows_in + r, 8)
                    spec_out[m, at // rows_in, 0, rows, lanes] = re
                    spec_out[m, at // rows_in, 1, rows, lanes] = im
            return c0

        lax.fori_loop(0, LANES // 8, tile_out, 0)

        for d in range(strips):
            for c in range(2):
                for e in range(2):
                    beside = d - 1 if e == 0 else d + 1
                    at_row = rows_in - 1 if e == 0 else 0
                    for b in range(lane_blocks):
                        if 0 <= beside < strips:
                            value = spec_out[m, beside, c, pl.ds(at_row, 1), pl.ds(b * LANES, LANES)]
                        else:
                            value = jnp.zeros((1, LANES), jnp.float32)
                        at = (c * 2 + e) * lane_blocks + b
                        edge_out[m, d, pl.ds(at, 1), :] = value

        for mask in lat_masks:
            to = lat_peer(mask)
            remote(
                edge_out.at[m, to], edge_in.at[m, lat], edge_send.at[m], edge_recv.at[m], (to, fr)
            ).start()
        pltpu.make_async_copy(edge_out.at[m, lat], edge_in.at[m, lat], edge_own.at[m]).start()

        def send_lines(i, c0):
            rows = piece_rows(i)
            for mask in lat_masks:
                to = lat_peer(mask)
                remote(
                    spec_out.at[m, to, :, rows, :], line_in.at[m, lat, :, rows, :],
                    line_send.at[m], line_recv.at[m, i], (to, fr),
                ).start()
            pltpu.make_async_copy(
                spec_out.at[m, lat, :, rows, :], line_in.at[m, lat, :, rows, :], line_own.at[m, i]
            ).start()
            return c0

        lax.fori_loop(0, pieces, send_lines, 0)
        return carry

    lax.fori_loop(0, members, shift, 0)

    def columns(z, rows):
        cells = []
        for k in range(factor):
            re, im = z[k, rows, pl.ds(0, LANES)], z[k, rows, pl.ds(LANES, LANES)]
            if k:
                c, s = tw_ref[0, pl.ds(k, 1), :], tw_ref[1, pl.ds(k, 1), :]
                re, im = re * c - im * s, im * c + re * s
            cells.append((re, im))
        return fft_list(cells, 1.0)

    def inverse_dot(x):
        high, low = split(x)
        return dot(high, m_inv[0]) + (dot(low, m_inv[0]) + dot(high, m_inv[1]))

    def edges(m):
        own = edge_in.at[m, lat]
        pltpu.make_async_copy(own, own, edge_own.at[m]).wait()
        some = edge_in.at[m, pl.ds(0, strips - 1)]
        remote(some, some, edge_send.at[m], edge_recv.at[m], (lat, fr)).wait_recv()
        ze[...] = jnp.zeros_like(ze)
        for k in range(factor):
            at = k * LANES
            b = (at % width) // LANES
            for c in range(2):
                for e in range(2):
                    row_at = (c * 2 + e) * lane_blocks + b
                    ze[k, pl.ds(e, 1), pl.ds(c * LANES, LANES)] = edge_in[
                        m, at // width, pl.ds(row_at, 1), :
                    ]
        y = inverse_dot(ze[...].reshape(factor * 8, 2 * LANES))
        ze[...] = y.reshape(factor, 8, 2 * LANES)
        for n, pair in enumerate(columns(ze, pl.ds(0, 8))):
            for c in range(2):
                field[c, pl.ds(7, 1), pl.ds(n * LANES, LANES)] = pair[c][0:1]
                field[c, pl.ds(8 + rows_in, 1), pl.ds(n * LANES, LANES)] = pair[c][1:2]

    def inverse_block(m, i):
        rows = piece_rows(i)
        own = line_in.at[m, lat, :, rows, :]
        pltpu.make_async_copy(own, own, line_own.at[m, i]).wait()
        some = line_in.at[m, pl.ds(0, strips - 1), :, rows, :]
        remote(some, some, line_send.at[m], line_recv.at[m, i], (lat, fr)).wait_recv()
        parts = []
        for k in range(factor):
            at = k * LANES
            cols = pl.ds(at % width, LANES)
            parts.append(
                jnp.concatenate(
                    [line_in[m, at // width, 0, rows, cols], line_in[m, at // width, 1, rows, cols]],
                    axis=1,
                )
            )
        y = inverse_dot(jnp.concatenate(parts, axis=0))
        zp[...] = y.reshape(factor, PIECE, 2 * LANES)

        def tile(t, c0):
            r = pl.multiple_of(t * 8, 8)
            at_field = pl.ds(pl.multiple_of(8 + i * PIECE + t * 8, 8), 8)
            for n, pair in enumerate(columns(zp, pl.ds(r, 8))):
                for c in range(2):
                    field[c, at_field, pl.ds(n * LANES, LANES)] = pair[c]
            return c0

        lax.fori_loop(0, PIECE // 8, tile, 0)

    column = lax.broadcasted_iota(jnp.int32, (PIECE, full), 1)

    def stencil(m, i):
        n = m * pieces + i
        slot = n % 2
        rows = piece_rows(i)

        @pl.when(n + 1 < members * pieces)
        def _():
            source_copy(n + 1).start()

        source_copy(n).wait()
        angular = 2.0 * math.pi * freq_step * freq_ref[m].astype(jnp.float32)
        ahead = 0.5 / (angular * mean)
        start = pl.multiple_of(i * PIECE, PIECE)
        centre, laplace = [], []
        for c in range(2):
            cells = field[c, pl.ds(start, PIECE + 16), :]
            mid = cells[8 : 8 + PIECE]
            up = pltpu.roll(cells, 1, 0)[8 : 8 + PIECE]
            down = pltpu.roll(cells, PIECE + 15, 0)[8 : 8 + PIECE]
            left = jnp.where(column == 0, 0.0, pltpu.roll(mid, 1, 1))
            right = jnp.where(column == full - 1, 0.0, pltpu.roll(mid, full - 1, 1))
            centre.append(mid)
            laplace.append(up + down + left + right - 4.0 * mid)
        slow_rows = jnp.concatenate([slow[p, rows, :] for p in range(groups)], axis=1)
        gain = (ahead - 0.5 / (angular * slow_rows)) * (depth_step / (grid_step * grid_step))
        new_re = centre[0] + gain * laplace[1]
        new_im = centre[1] - gain * laplace[0]
        fresh[0, m, rows, :] = new_re
        fresh[1, m, rows, :] = new_im
        term = (new_re * source[slot, 0] + new_im * source[slot, 1]) * (
            1.0 / math.sqrt(batch_total)
        )
        for p in range(groups):
            part = term[:, p * part_width : (p + 1) * part_width]

            @pl.when(m == 0)
            def _():
                terms[p, rows, :] = part

            @pl.when(m > 0)
            def _():
                terms[p, rows, :] = terms[p, rows, :] + part

        @pl.when(m == members - 1)
        def _():
            for mask in freq_masks:
                to = freq_peer(mask)
                remote(
                    terms.at[to, rows, :], terms_in.at[fr, rows, :], term_send, term_recv,
                    (lat, to),
                ).start()
            terms_in[fr, rows, :] = terms[fr, rows, :]

    def finish(n, carry):
        m, j = n // (pieces + 1), n % (pieces + 1)

        @pl.when(j == 0)
        def _():
            edges(m)

        @pl.when(j < pieces)
        def _():
            inverse_block(m, j)

        @pl.when(j > 0)
        def _():
            stencil(m, j - 1)

        return carry

    lax.fori_loop(0, members * (pieces + 1), finish, 0)
    some = slow.at[pl.ds(0, groups - 1)]
    remote(some, some, slow_send, slow_recv.at[0], (lat, fr)).wait_send()
    some = terms.at[pl.ds(0, groups - 1)]
    remote(some, some, term_send, term_recv, (lat, fr)).wait()
    some = stat_in.at[pl.ds(0, strips - 1)]
    remote(some, some, stat_send, stat_recv, (lat, fr)).wait_send()
    for m in range(members):
        some = spec_out.at[m, pl.ds(0, strips - 1)]
        remote(some, some, line_send.at[m], line_recv.at[m, 0], (lat, fr)).wait_send()
        some = edge_out.at[m, pl.ds(0, strips - 1)]
        remote(some, some, edge_send.at[m], edge_recv.at[m], (lat, fr)).wait_send()


def write_kernel(fresh, terms, field_hbm, image_hbm, image, field_sem, image_sem):
    rows = fresh.shape[2]
    part = rows // 4
    for r in range(0, rows, part):
        for c in range(fresh.shape[0]):
            for m in range(fresh.shape[1]):
                pltpu.make_async_copy(
                    fresh.at[c, m, pl.ds(r, part)], field_hbm.at[c, m, pl.ds(r, part)], field_sem
                ).start()
    total = terms[0]
    for p in range(1, terms.shape[0]):
        total = total + terms[p]
    image[...] = total
    copy = pltpu.make_async_copy(image, image_hbm, image_sem)
    copy.start()
    copy.wait()
    pltpu.make_async_copy(fresh, field_hbm, field_sem).wait()


def local(wavefield, source_field, slowness, freq_index):
    _, members, rows, full = wavefield.shape
    strips, groups = lax.axis_size("lat"), lax.axis_size("freq")
    width = full // strips
    factor = full // LANES
    part_width = full // groups
    blocks, pieces = rows // CHUNK, rows // PIECE
    tw = twiddle(full)
    tw_row = jnp.asarray(tw)
    tw_x = jnp.asarray(np.ascontiguousarray(np.broadcast_to(tw[..., None], tw.shape + (LANES,))))
    right_fwd, right_inv = dft_tables(-1.0), dft_tables(1.0)
    m_fwd, m_inv = split_table(right_fwd), split_table(right_inv)
    m_both = jnp.concatenate(
        [split_table(np.ascontiguousarray(right_fwd.T)), split_table(np.ascontiguousarray(right_inv.T))]
    )
    edge_rows = max(8, 4 * width // LANES)
    far = pl.BlockSpec(memory_space=pltpu.HBM)
    anywhere = pl.BlockSpec(memory_space=pl.ANY)
    inside = pl.BlockSpec(memory_space=pltpu.VMEM)
    f32 = jnp.float32
    dma = pltpu.SemaphoreType.DMA
    fresh, terms = pl.pallas_call(
        functools.partial(step_kernel, batch_total=members * groups),
        in_specs=[far] * 9,
        out_specs=[inside, inside],
        out_shape=[
            pltpu.VMEM((2, members, rows, full), f32),
            pltpu.VMEM((groups, rows, part_width), f32),
        ],
        scratch_shapes=[
            pltpu.VMEM((members, strips, 2, rows, width), f32),
            pltpu.VMEM((members, strips, 2, rows, width), f32),
            pltpu.VMEM((members, strips, 2, rows, width), f32),
            pltpu.VMEM((members, strips, edge_rows, LANES), f32),
            pltpu.VMEM((members, strips, edge_rows, LANES), f32),
            pltpu.VMEM((1, LANES), f32),
            pltpu.VMEM((strips, 1, LANES), f32),
            pltpu.VMEM((groups, rows, part_width), f32),
            pltpu.VMEM((groups, rows, part_width), f32),
            pltpu.VMEM((factor, 2 * LANES, width), f32),
            pltpu.VMEM((factor, CHUNK, 2 * LANES), f32),
            pltpu.VMEM((factor, PIECE, 2 * LANES), f32),
            pltpu.VMEM((factor, 8, 2 * LANES), f32),
            pltpu.VMEM((2, rows + 16, full), f32),
            pltpu.VMEM((2, 2, CHUNK, full), f32),
            pltpu.VMEM((2, 2, PIECE, full), f32),
            pltpu.VMEM(tw_x.shape, f32),
            pltpu.VMEM(tw_row.shape, f32),
            pltpu.VMEM(m_fwd.shape, m_fwd.dtype),
            pltpu.VMEM(m_both.shape, m_both.dtype),
            pltpu.VMEM(m_inv.shape, m_inv.dtype),
            pltpu.SMEM((members,), jnp.int32),
            dma((2,)), dma((2,)), dma((3,)), dma((3,)), dma,
            dma, dma((blocks,)),
            dma((members,)), dma((members, strips)), dma((members,)),
            dma((members,)), dma((members, pieces)), dma((members, pieces)),
            dma((members,)), dma((members,)), dma((members,)),
            dma, dma,
            dma, dma,
        ],
        compiler_params=pltpu.CompilerParams(
            collective_id=0, has_side_effects=True, vmem_limit_bytes=VMEM_BYTES
        ),
        cost_estimate=pl.CostEstimate(
            flops=13_000_000_000, bytes_accessed=26_000_000, transcendentals=0
        ),
        name="depth_step",
    )(freq_index, wavefield, source_field, slowness, tw_x, tw_row, m_fwd, m_both, m_inv)
    return pl.pallas_call(
        write_kernel,
        in_specs=[inside, inside],
        out_specs=[anywhere, anywhere],
        out_shape=[
            jax.ShapeDtypeStruct((2, members, rows, full), f32),
            jax.ShapeDtypeStruct((rows, part_width), f32),
        ],
        scratch_shapes=[pltpu.VMEM((rows, part_width), f32), dma, dma],
        compiler_params=pltpu.CompilerParams(vmem_limit_bytes=SMALL_BYTES),
        cost_estimate=pl.CostEstimate(flops=400_000, bytes_accessed=8_400_000, transcendentals=0),
        name="write_out",
    )(fresh, terms)


def solution(mesh):
    return jax.shard_map(
        local,
        mesh=mesh,
        in_specs=(
            P(None, "freq", "lat", None),
            P(None, "freq", "lat", None),
            P("lat", "freq"),
            P("freq"),
        ),
        out_specs=(P(None, "freq", "lat", None), P("lat", "freq")),
        check_vma=False,
    )
```

```python
import functools
import math

import jax
import jax.numpy as jnp
import numpy as np
from jax import lax
from jax.experimental import pallas as pl
from jax.experimental.pallas import tpu as pltpu
from jax.sharding import PartitionSpec as P

depth_step = 10.0
grid_step = 25.0
freq_step = 0.0625
LANES = 128
CHUNK = 8
PIECE = 8
AHEAD = 2
VMEM_BYTES = 52 * 1024 * 1024
SMALL_BYTES = 4 * 1024 * 1024
MESH = pl.DeviceIdType.MESH


def dft_tables(sign):
    i = np.arange(LANES)
    ang = 2.0 * math.pi / LANES * ((i[:, None] * i[None, :]) % LANES)
    c, s = np.cos(ang), sign * np.sin(ang)
    return np.block([[c, s], [-s, c]])


def split_table(table):
    high = jnp.asarray(table.astype(np.float32)).astype(jnp.bfloat16)
    high64 = np.asarray(table.astype(np.float32).astype(jnp.bfloat16)).astype(np.float64)
    low = (table - high64).astype(np.float32).astype(jnp.bfloat16)
    return jnp.stack([high, jnp.asarray(low)])


def twiddle(count):
    factor = count // LANES
    k, n = np.arange(factor), np.arange(LANES)
    ang = 2.0 * math.pi / count * ((k[:, None] * n[None, :]) % count)
    return np.stack([np.cos(ang), np.sin(ang)]).astype(np.float32)


def fft_list(values, sign):
    count = len(values)
    if count == 1:
        return values
    even, odd = fft_list(values[0::2], sign), fft_list(values[1::2], sign)
    low, high = [], []
    for k in range(count // 2):
        (er, ei), (r, i) = even[k], odd[k]
        if k == 0:
            tr, ti = r, i
        elif 4 * k == count:
            tr, ti = (-i, r) if sign > 0 else (i, -r)
        else:
            c = math.cos(2.0 * math.pi * k / count)
            s = sign * math.sin(2.0 * math.pi * k / count)
            if abs(abs(c) - abs(s)) < 1e-9:
                h = math.sqrt(0.5)
                sc, ss = (1 if c > 0 else -1), (1 if s > 0 else -1)
                tr = h * (r - i) if sc * ss > 0 else h * (r + i)
                ti = h * (i + r) if sc * ss > 0 else h * (i - r)
                if sc < 0:
                    tr, ti = -tr, -ti
            else:
                tr, ti = c * r - s * i, c * i + s * r
        low.append((er + tr, ei + ti))
        high.append((er - tr, ei - ti))
    return low + high


def sin_cos(angle):
    turns = jnp.round(angle * (0.5 / math.pi))
    r = angle - turns * 6.28125 - turns * (2.0 * math.pi - 6.28125)
    r2 = r * r
    s = jnp.full_like(r, 1.0 / math.factorial(17))
    for n in range(15, 0, -2):
        s = s * r2 + ((-1) ** (n // 2)) / math.factorial(n)
    c = jnp.full_like(r, -1.0 / math.factorial(18))
    for n in range(16, -1, -2):
        c = c * r2 + ((-1) ** (n // 2)) / math.factorial(n)
    return s * r, c


def split(x):
    high = x.astype(jnp.bfloat16)
    return high, (x - high.astype(jnp.float32)).astype(jnp.bfloat16)


def dot(a, b):
    return jnp.dot(a, b, preferred_element_type=jnp.float32)


def flipped(index, mask, count):
    other, bit = index, 1
    while bit < count:
        if mask & bit:
            other = other + bit * (1 - 2 * ((index // bit) % 2))
        bit *= 2
    return other


def step_kernel(
    freq_hbm, wave_hbm, src_hbm, slow_hbm, twx_hbm, tw_hbm, fwd_hbm, both_hbm, inv_hbm,
    fresh, terms_in,
    spec_out, spec_in, line_in, edge_out, edge_in, stat_out, stat_in,
    slow, terms, zs, zc, zp, ze, field, wave, source,
    twx, tw_ref, m_fwd, m_both, m_inv, freq_ref,
    wave_sem, source_sem, early_sem, late_sem, own_sem,
    slow_send, slow_recv, spec_send, spec_recv, spec_own, line_send, line_recv, line_own,
    edge_send, edge_recv, edge_own, stat_send, stat_recv, term_send, term_recv, greet,
    *, batch_total,
):
    members, strips, rows_in, width = (spec_out.shape[i] for i in (0, 1, 3, 4))
    groups, part_width = slow.shape[0], slow.shape[2]
    full = strips * width
    factor = full // LANES
    count = rows_in * strips
    blocks, pieces = rows_in // CHUNK, rows_in // PIECE
    lane_blocks = width // LANES
    lat, fr = lax.axis_index("lat"), lax.axis_index("freq")
    lat_masks = sorted(range(1, strips), key=lambda m: -m)
    freq_masks = list(range(1, groups))

    def lat_peer(mask):
        return flipped(lat, mask, strips)

    def freq_peer(mask):
        return flipped(fr, mask, groups)

    def chunk_rows(i):
        return pl.ds(pl.multiple_of(i * CHUNK, CHUNK), CHUNK)

    def piece_rows(i):
        return pl.ds(pl.multiple_of(i * PIECE, PIECE), PIECE)

    def remote(a, b, send, recv, to):
        return pltpu.make_async_remote_copy(
            src_ref=a, dst_ref=b, send_sem=send, recv_sem=recv, device_id=to, device_id_type=MESH
        )

    def wave_copy(n):
        rows = chunk_rows(n % blocks)
        return pltpu.make_async_copy(
            wave_hbm.at[:, n // blocks, rows, :], wave.at[n % 2], wave_sem.at[n % 2]
        )

    def source_copy(n):
        rows = piece_rows(n % pieces)
        return pltpu.make_async_copy(
            src_hbm.at[:, n // pieces, rows, :], source.at[n % 2], source_sem.at[n % 2]
        )

    barrier = pltpu.get_barrier_semaphore()
    for mask in freq_masks:
        pl.semaphore_signal(barrier, inc=1, device_id=(lat, freq_peer(mask)), device_id_type=MESH)
    lat_bits = [bit for bit in lat_masks if bit & (bit - 1) == 0]
    for mask in lat_bits:
        pl.semaphore_signal(barrier, inc=1, device_id=(lat_peer(mask), fr), device_id_type=MESH)

    own_slow = pltpu.make_async_copy(slow_hbm, slow.at[fr], own_sem)
    own_slow.start()
    wave_copy(0).start()
    early = [
        pltpu.make_async_copy(a, b, early_sem.at[i])
        for i, (a, b) in enumerate(((tw_hbm, tw_ref), (fwd_hbm, m_fwd), (freq_hbm, freq_ref)))
    ]
    late = [
        pltpu.make_async_copy(a, b, late_sem.at[i])
        for i, (a, b) in enumerate(((twx_hbm, twx), (both_hbm, m_both), (inv_hbm, m_inv)))
    ]
    for copy in early:
        copy.start()
    pl.semaphore_wait(barrier, len(freq_masks) + len(lat_bits))

    def send_slow(i, carry):
        rows = chunk_rows(i)
        for mask in freq_masks:
            remote(
                slow.at[fr, rows, :], slow.at[fr, rows, :], slow_send, slow_recv.at[i],
                (lat, freq_peer(mask)),
            ).start()
        return carry

    own_slow.wait()
    lax.fori_loop(0, min(AHEAD, blocks), send_slow, 0)
    for stage in range(len(lat_bits) - 1):
        for mask in lat_bits:
            pl.semaphore_signal(
                greet.at[stage], inc=1, device_id=(lat_peer(mask), fr), device_id_type=MESH
            )
        pl.semaphore_wait(greet.at[stage], len(lat_bits))
    for copy in early:
        copy.wait()

    def forward(n, carry):
        m, i = n // blocks, n % blocks
        rows = chunk_rows(i)

        @pl.when(n + 1 < members * blocks)
        def _():
            wave_copy(n + 1).start()

        @pl.when(n + AHEAD < blocks)
        def _():
            send_slow(n + AHEAD, 0)

        @pl.when(n < blocks)
        def _():
            some = slow.at[pl.ds(0, groups - 1), rows, :]
            remote(some, some, slow_send, slow_recv.at[i], (lat, fr)).wait_recv()

        wave_copy(n).wait()
        scale = 2.0 * math.pi * freq_step * freq_ref[m].astype(jnp.float32) * depth_step
        slot = n % 2

        def tile(t, c0):
            r = pl.multiple_of(t * 8, 8)
            at_slow = pl.ds(pl.multiple_of(i * CHUNK + t * 8, 8), 8)
            cells = []
            for k in range(factor):
                at = k * LANES
                s = slow[at // part_width, at_slow, pl.ds(at % part_width, LANES)]
                sn, cs = sin_cos(s * scale)
                re = wave[slot, 0, pl.ds(r, 8), pl.ds(at, LANES)]
                im = wave[slot, 1, pl.ds(r, 8), pl.ds(at, LANES)]
                cells.append((re * cs - im * sn, re * sn + im * cs))
            for k, (re, im) in enumerate(fft_list(cells, -1.0)):
                if k:
                    c, s = tw_ref[0, pl.ds(k, 1), :], tw_ref[1, pl.ds(k, 1), :]
                    re, im = re * c + im * s, im * c - re * s
                zc[k, pl.ds(r, 8), pl.ds(0, LANES)] = re
                zc[k, pl.ds(r, 8), pl.ds(LANES, LANES)] = im
            return c0

        lax.fori_loop(0, CHUNK // 8, tile, 0)
        high, low = split(zc[...].reshape(factor * CHUNK, 2 * LANES))
        y = dot(high, m_fwd[0]) + (dot(low, m_fwd[0]) + dot(high, m_fwd[1]))
        y = y.reshape(factor, CHUNK, 2 * LANES)
        for k in range(factor):
            at = k * LANES
            cols = pl.ds(at % width, LANES)
            spec_out[m, at // width, 0, rows, cols] = y[k, :, :LANES]
            spec_out[m, at // width, 1, rows, cols] = y[k, :, LANES:]
        for mask in lat_masks:
            to = lat_peer(mask)
            remote(
                spec_out.at[m, to, :, rows, :], spec_in.at[m, lat, :, rows, :],
                spec_send.at[m], spec_recv.at[m, lat], (to, fr),
            ).start()
        pltpu.make_async_copy(
            spec_out.at[m, lat, :, rows, :], spec_in.at[m, lat, :, rows, :], spec_own.at[m]
        ).start()

        @pl.when(n == blocks - 1)
        def _():
            def add(t, sums):
                at_slow = pl.ds(pl.multiple_of(t * 8, 8), 8)
                for p in range(groups):
                    for at in range(0, part_width, LANES):
                        sums = sums + slow[p, at_slow, pl.ds(at, LANES)]
                return sums

            total = lax.fori_loop(0, rows_in // 8, add, jnp.zeros((8, LANES), jnp.float32))
            total = jnp.sum(total, axis=0, keepdims=True)
            stat_out[...] = total
            stat_in[lat] = total
            for mask in lat_masks:
                remote(
                    stat_out, stat_in.at[lat], stat_send, stat_recv, (lat_peer(mask), fr)
                ).start()

        return carry

    lax.fori_loop(0, members * blocks, forward, 0)

    source_copy(0).start()
    for copy in late:
        copy.start()
    some = stat_in.at[pl.ds(0, strips - 1)]
    remote(some, some, stat_send, stat_recv, (lat, fr)).wait_recv()
    for copy in late:
        copy.wait()
    mean = jnp.sum(stat_in[...]) * (1.0 / (count * full))

    def shift(m, carry):
        own = spec_in.at[m, lat]
        pltpu.make_async_copy(own, own, spec_own.at[m]).wait()
        for mask in lat_masks:
            peer = lat_peer(mask)
            whole_in = spec_in.at[m, peer]
            remote(whole_in, whole_in, spec_send.at[m], spec_recv.at[m, peer], (lat, fr)).wait_recv()

        def tile_in(t, c0):
            r = pl.multiple_of(t * 8, 8)
            for lane in range(0, width, LANES):
                lanes = pl.ds(lane, LANES)
                cells = []
                for n in range(factor):
                    at = n * LANES
                    rows = pl.ds(at % rows_in + r, 8)
                    cells.append(
                        (spec_in[m, at // rows_in, 0, rows, lanes],
                         spec_in[m, at // rows_in, 1, rows, lanes])
                    )
                for k, (re, im) in enumerate(fft_list(cells, -1.0)):
                    if k:
                        c, s = twx[0, k, pl.ds(r, 8), :], twx[1, k, pl.ds(r, 8), :]
                        re, im = re * c + im * s, im * c - re * s
                    zs[k, pl.ds(r, 8), lanes] = re
                    zs[k, pl.ds(LANES + r, 8), lanes] = im
            return c0

        lax.fori_loop(0, LANES // 8, tile_in, 0)

        angular_mean = 2.0 * math.pi * freq_step * freq_ref[m].astype(jnp.float32) * mean
        flat = angular_mean * depth_step
        place = lat * width + lax.broadcasted_iota(jnp.int32, (LANES, width), 1)
        index_y = place // LANES + factor * (place % LANES)
        signed_y = jnp.where(index_y < full // 2, index_y, index_y - full)
        wave_y = 2.0 * math.pi / (full * grid_step) * signed_y.astype(jnp.float32)
        rest = angular_mean * angular_mean - wave_y * wave_y
        row = lax.broadcasted_iota(jnp.int32, (LANES, width), 0)

        def product(k, c0):
            high, low = split(zs[k])
            y = dot(m_both[0], high) + (dot(m_both[0], low) + dot(m_both[1], high))
            index_x = k + factor * row
            signed_x = jnp.where(index_x < count // 2, index_x, index_x - count)
            wave_x = 2.0 * math.pi / (count * grid_step) * signed_x.astype(jnp.float32)
            vertical = rest - wave_x * wave_x
            size = jnp.sqrt(jnp.abs(vertical)) * depth_step
            damping = jnp.where(vertical < 0.0, jnp.exp(-size), 1.0) * (1.0 / (count * full))
            sn, cs = sin_cos(jnp.where(vertical > 0.0, size, 0.0) - flat)
            tr, ti = damping * cs, damping * sn
            re, im = y[:LANES], y[LANES:]
            z = jnp.concatenate([re * tr - im * ti, re * ti + im * tr], axis=0)
            high, low = split(z)
            zs[k] = dot(m_both[2], high) + (dot(m_both[2], low) + dot(m_both[3], high))
            return c0

        lax.fori_loop(0, factor, product, 0)
        some = spec_out.at[m, pl.ds(0, strips - 1)]
        remote(some, some, spec_send.at[m], spec_recv.at[m, 0], (lat, fr)).wait_send()

        def tile_out(t, c0):
            r = pl.multiple_of(t * 8, 8)
            for lane in range(0, width, LANES):
                lanes = pl.ds(lane, LANES)
                cells = []
                for k in range(factor):
                    re, im = zs[k, pl.ds(r, 8), lanes], zs[k, pl.ds(LANES + r, 8), lanes]
                    if k:
                        c, s = twx[0, k, pl.ds(r, 8), :], twx[1, k, pl.ds(r, 8), :]
                        re, im = re * c - im * s, im * c + re * s
                    cells.append((re, im))
                for n, (re, im) in enumerate(fft_list(cells, 1.0)):
                    at = n * LANES
                    rows = pl.ds(at % rows_in + r, 8)
                    spec_out[m, at // rows_in, 0, rows, lanes] = re
                    spec_out[m, at // rows_in, 1, rows, lanes] = im
            return c0

        lax.fori_loop(0, LANES // 8, tile_out, 0)

        for d in range(strips):
            for c in range(2):
                for e in range(2):
                    beside = d - 1 if e == 0 else d + 1
                    at_row = rows_in - 1 if e == 0 else 0
                    for b in range(lane_blocks):
                        if 0 <= beside < strips:
                            value = spec_out[m, beside, c, pl.ds(at_row, 1), pl.ds(b * LANES, LANES)]
                        else:
                            value = jnp.zeros((1, LANES), jnp.float32)
                        at = (c * 2 + e) * lane_blocks + b
                        edge_out[m, d, pl.ds(at, 1), :] = value

        for mask in lat_masks:
            to = lat_peer(mask)
            remote(
                edge_out.at[m, to], edge_in.at[m, lat], edge_send.at[m], edge_recv.at[m], (to, fr)
            ).start()
        pltpu.make_async_copy(edge_out.at[m, lat], edge_in.at[m, lat], edge_own.at[m]).start()

        def send_lines(i, c0):
            rows = piece_rows(i)
            for mask in lat_masks:
                to = lat_peer(mask)
                remote(
                    spec_out.at[m, to, :, rows, :], line_in.at[m, lat, :, rows, :],
                    line_send.at[m], line_recv.at[m, i], (to, fr),
                ).start()
            pltpu.make_async_copy(
                spec_out.at[m, lat, :, rows, :], line_in.at[m, lat, :, rows, :], line_own.at[m, i]
            ).start()
            return c0

        lax.fori_loop(0, pieces, send_lines, 0)
        return carry

    lax.fori_loop(0, members, shift, 0)

    def columns(z, rows):
        cells = []
        for k in range(factor):
            re, im = z[k, rows, pl.ds(0, LANES)], z[k, rows, pl.ds(LANES, LANES)]
            if k:
                c, s = tw_ref[0, pl.ds(k, 1), :], tw_ref[1, pl.ds(k, 1), :]
                re, im = re * c - im * s, im * c + re * s
            cells.append((re, im))
        return fft_list(cells, 1.0)

    def inverse_dot(x):
        high, low = split(x)
        return dot(high, m_inv[0]) + (dot(low, m_inv[0]) + dot(high, m_inv[1]))

    def edges(m):
        own = edge_in.at[m, lat]
        pltpu.make_async_copy(own, own, edge_own.at[m]).wait()
        some = edge_in.at[m, pl.ds(0, strips - 1)]
        remote(some, some, edge_send.at[m], edge_recv.at[m], (lat, fr)).wait_recv()
        ze[...] = jnp.zeros_like(ze)
        for k in range(factor):
            at = k * LANES
            b = (at % width) // LANES
            for c in range(2):
                for e in range(2):
                    row_at = (c * 2 + e) * lane_blocks + b
                    ze[k, pl.ds(e, 1), pl.ds(c * LANES, LANES)] = edge_in[
                        m, at // width, pl.ds(row_at, 1), :
                    ]
        y = inverse_dot(ze[...].reshape(factor * 8, 2 * LANES))
        ze[...] = y.reshape(factor, 8, 2 * LANES)
        for n, pair in enumerate(columns(ze, pl.ds(0, 8))):
            for c in range(2):
                field[c, pl.ds(7, 1), pl.ds(n * LANES, LANES)] = pair[c][0:1]
                field[c, pl.ds(8 + rows_in, 1), pl.ds(n * LANES, LANES)] = pair[c][1:2]

    def inverse_block(m, i):
        rows = piece_rows(i)
        own = line_in.at[m, lat, :, rows, :]
        pltpu.make_async_copy(own, own, line_own.at[m, i]).wait()
        some = line_in.at[m, pl.ds(0, strips - 1), :, rows, :]
        remote(some, some, line_send.at[m], line_recv.at[m, i], (lat, fr)).wait_recv()
        parts = []
        for k in range(factor):
            at = k * LANES
            cols = pl.ds(at % width, LANES)
            parts.append(
                jnp.concatenate(
                    [line_in[m, at // width, 0, rows, cols], line_in[m, at // width, 1, rows, cols]],
                    axis=1,
                )
            )
        y = inverse_dot(jnp.concatenate(parts, axis=0))
        zp[...] = y.reshape(factor, PIECE, 2 * LANES)

        def tile(t, c0):
            r = pl.multiple_of(t * 8, 8)
            at_field = pl.ds(pl.multiple_of(8 + i * PIECE + t * 8, 8), 8)
            for n, pair in enumerate(columns(zp, pl.ds(r, 8))):
                for c in range(2):
                    field[c, at_field, pl.ds(n * LANES, LANES)] = pair[c]
            return c0

        lax.fori_loop(0, PIECE // 8, tile, 0)

    column = lax.broadcasted_iota(jnp.int32, (PIECE, full), 1)

    def stencil(m, i):
        n = m * pieces + i
        slot = n % 2
        rows = piece_rows(i)

        @pl.when(n + 1 < members * pieces)
        def _():
            source_copy(n + 1).start()

        source_copy(n).wait()
        angular = 2.0 * math.pi * freq_step * freq_ref[m].astype(jnp.float32)
        ahead = 0.5 / (angular * mean)
        start = pl.multiple_of(i * PIECE, PIECE)
        centre, laplace = [], []
        for c in range(2):
            cells = field[c, pl.ds(start, PIECE + 16), :]
            mid = cells[8 : 8 + PIECE]
            up = pltpu.roll(cells, 1, 0)[8 : 8 + PIECE]
            down = pltpu.roll(cells, PIECE + 15, 0)[8 : 8 + PIECE]
            left = jnp.where(column == 0, 0.0, pltpu.roll(mid, 1, 1))
            right = jnp.where(column == full - 1, 0.0, pltpu.roll(mid, full - 1, 1))
            centre.append(mid)
            laplace.append(up + down + left + right - 4.0 * mid)
        slow_rows = jnp.concatenate([slow[p, rows, :] for p in range(groups)], axis=1)
        gain = (ahead - 0.5 / (angular * slow_rows)) * (depth_step / (grid_step * grid_step))
        new_re = centre[0] + gain * laplace[1]
        new_im = centre[1] - gain * laplace[0]
        fresh[0, m, rows, :] = new_re
        fresh[1, m, rows, :] = new_im
        term = (new_re * source[slot, 0] + new_im * source[slot, 1]) * (
            1.0 / math.sqrt(batch_total)
        )
        for p in range(groups):
            part = term[:, p * part_width : (p + 1) * part_width]

            @pl.when(m == 0)
            def _():
                terms[p, rows, :] = part

            @pl.when(m > 0)
            def _():
                terms[p, rows, :] = terms[p, rows, :] + part

        @pl.when(m == members - 1)
        def _():
            for mask in freq_masks:
                to = freq_peer(mask)
                remote(
                    terms.at[to, rows, :], terms_in.at[fr, rows, :], term_send, term_recv,
                    (lat, to),
                ).start()
            terms_in[fr, rows, :] = terms[fr, rows, :]

    def finish(n, carry):
        m, j = n // (pieces + 1), n % (pieces + 1)

        @pl.when(j == 0)
        def _():
            edges(m)

        @pl.when(j < pieces)
        def _():
            inverse_block(m, j)

        @pl.when(j > 0)
        def _():
            stencil(m, j - 1)

        return carry

    lax.fori_loop(0, members * (pieces + 1), finish, 0)
    some = slow.at[pl.ds(0, groups - 1)]
    remote(some, some, slow_send, slow_recv.at[0], (lat, fr)).wait_send()
    some = terms.at[pl.ds(0, groups - 1)]
    remote(some, some, term_send, term_recv, (lat, fr)).wait()
    some = stat_in.at[pl.ds(0, strips - 1)]
    remote(some, some, stat_send, stat_recv, (lat, fr)).wait_send()
    for m in range(members):
        some = spec_out.at[m, pl.ds(0, strips - 1)]
        remote(some, some, line_send.at[m], line_recv.at[m, 0], (lat, fr)).wait_send()
        some = edge_out.at[m, pl.ds(0, strips - 1)]
        remote(some, some, edge_send.at[m], edge_recv.at[m], (lat, fr)).wait_send()


def write_kernel(fresh, terms, field_hbm, image_hbm, image, field_sem, image_sem):
    rows = fresh.shape[2]
    part = rows // 4
    for r in range(0, rows, part):
        for c in range(fresh.shape[0]):
            for m in range(fresh.shape[1]):
                pltpu.make_async_copy(
                    fresh.at[c, m, pl.ds(r, part)], field_hbm.at[c, m, pl.ds(r, part)], field_sem
                ).start()
    total = terms[0]
    for p in range(1, terms.shape[0]):
        total = total + terms[p]
    image[...] = total
    copy = pltpu.make_async_copy(image, image_hbm, image_sem)
    copy.start()
    copy.wait()
    pltpu.make_async_copy(fresh, field_hbm, field_sem).wait()


def local(wavefield, source_field, slowness, freq_index):
    _, members, rows, full = wavefield.shape
    strips, groups = lax.axis_size("lat"), lax.axis_size("freq")
    width = full // strips
    factor = full // LANES
    part_width = full // groups
    blocks, pieces = rows // CHUNK, rows // PIECE
    tw = twiddle(full)
    tw_row = jnp.asarray(tw)
    tw_x = jnp.asarray(np.ascontiguousarray(np.broadcast_to(tw[..., None], tw.shape + (LANES,))))
    right_fwd, right_inv = dft_tables(-1.0), dft_tables(1.0)
    m_fwd, m_inv = split_table(right_fwd), split_table(right_inv)
    m_both = jnp.concatenate(
        [split_table(np.ascontiguousarray(right_fwd.T)), split_table(np.ascontiguousarray(right_inv.T))]
    )
    edge_rows = max(8, 4 * width // LANES)
    far = pl.BlockSpec(memory_space=pltpu.HBM)
    anywhere = pl.BlockSpec(memory_space=pl.ANY)
    inside = pl.BlockSpec(memory_space=pltpu.VMEM)
    f32 = jnp.float32
    dma = pltpu.SemaphoreType.DMA
    fresh, terms = pl.pallas_call(
        functools.partial(step_kernel, batch_total=members * groups),
        in_specs=[far] * 9,
        out_specs=[inside, inside],
        out_shape=[
            pltpu.VMEM((2, members, rows, full), f32),
            pltpu.VMEM((groups, rows, part_width), f32),
        ],
        scratch_shapes=[
            pltpu.VMEM((members, strips, 2, rows, width), f32),
            pltpu.VMEM((members, strips, 2, rows, width), f32),
            pltpu.VMEM((members, strips, 2, rows, width), f32),
            pltpu.VMEM((members, strips, edge_rows, LANES), f32),
            pltpu.VMEM((members, strips, edge_rows, LANES), f32),
            pltpu.VMEM((1, LANES), f32),
            pltpu.VMEM((strips, 1, LANES), f32),
            pltpu.VMEM((groups, rows, part_width), f32),
            pltpu.VMEM((groups, rows, part_width), f32),
            pltpu.VMEM((factor, 2 * LANES, width), f32),
            pltpu.VMEM((factor, CHUNK, 2 * LANES), f32),
            pltpu.VMEM((factor, PIECE, 2 * LANES), f32),
            pltpu.VMEM((factor, 8, 2 * LANES), f32),
            pltpu.VMEM((2, rows + 16, full), f32),
            pltpu.VMEM((2, 2, CHUNK, full), f32),
            pltpu.VMEM((2, 2, PIECE, full), f32),
            pltpu.VMEM(tw_x.shape, f32),
            pltpu.VMEM(tw_row.shape, f32),
            pltpu.VMEM(m_fwd.shape, m_fwd.dtype),
            pltpu.VMEM(m_both.shape, m_both.dtype),
            pltpu.VMEM(m_inv.shape, m_inv.dtype),
            pltpu.SMEM((members,), jnp.int32),
            dma((2,)), dma((2,)), dma((3,)), dma((3,)), dma,
            dma, dma((blocks,)),
            dma((members,)), dma((members, strips)), dma((members,)),
            dma((members,)), dma((members, pieces)), dma((members, pieces)),
            dma((members,)), dma((members,)), dma((members,)),
            dma, dma,
            dma, dma,
            pltpu.SemaphoreType.REGULAR((max(strips.bit_length() - 2, 1),)),
        ],
        compiler_params=pltpu.CompilerParams(
            collective_id=0, has_side_effects=True, vmem_limit_bytes=VMEM_BYTES
        ),
        cost_estimate=pl.CostEstimate(
            flops=13_000_000_000, bytes_accessed=26_000_000, transcendentals=0
        ),
        name="depth_step",
    )(freq_index, wavefield, source_field, slowness, tw_x, tw_row, m_fwd, m_both, m_inv)
    return pl.pallas_call(
        write_kernel,
        in_specs=[inside, inside],
        out_specs=[anywhere, anywhere],
        out_shape=[
            jax.ShapeDtypeStruct((2, members, rows, full), f32),
            jax.ShapeDtypeStruct((rows, part_width), f32),
        ],
        scratch_shapes=[pltpu.VMEM((rows, part_width), f32), dma, dma],
        compiler_params=pltpu.CompilerParams(vmem_limit_bytes=SMALL_BYTES),
        cost_estimate=pl.CostEstimate(flops=400_000, bytes_accessed=8_400_000, transcendentals=0),
        name="write_out",
    )(fresh, terms)


def solution(mesh):
    return jax.shard_map(
        local,
        mesh=mesh,
        in_specs=(
            P(None, "freq", "lat", None),
            P(None, "freq", "lat", None),
            P("lat", "freq"),
            P("freq"),
        ),
        out_specs=(P(None, "freq", "lat", None), P("lat", "freq")),
        check_vma=False,
    )
```

```python
import functools
import math

import jax
import jax.numpy as jnp
import numpy as np
from jax import lax
from jax.experimental import pallas as pl
from jax.experimental.pallas import tpu as pltpu
from jax.sharding import PartitionSpec as P

depth_step = 10.0
grid_step = 25.0
freq_step = 0.0625
LANES = 128
CHUNK = 8
PIECE = 8
AHEAD = 2
VMEM_BYTES = 52 * 1024 * 1024
SMALL_BYTES = 4 * 1024 * 1024
MESH = pl.DeviceIdType.MESH


def dft_tables(sign):
    i = np.arange(LANES)
    ang = 2.0 * math.pi / LANES * ((i[:, None] * i[None, :]) % LANES)
    c, s = np.cos(ang), sign * np.sin(ang)
    return np.block([[c, s], [-s, c]])


def split_table(table):
    high = jnp.asarray(table.astype(np.float32)).astype(jnp.bfloat16)
    high64 = np.asarray(table.astype(np.float32).astype(jnp.bfloat16)).astype(np.float64)
    low = (table - high64).astype(np.float32).astype(jnp.bfloat16)
    return jnp.stack([high, jnp.asarray(low)])


def twiddle(count):
    factor = count // LANES
    k, n = np.arange(factor), np.arange(LANES)
    ang = 2.0 * math.pi / count * ((k[:, None] * n[None, :]) % count)
    return np.stack([np.cos(ang), np.sin(ang)]).astype(np.float32)


def fft_list(values, sign):
    count = len(values)
    if count == 1:
        return values
    even, odd = fft_list(values[0::2], sign), fft_list(values[1::2], sign)
    low, high = [], []
    for k in range(count // 2):
        (er, ei), (r, i) = even[k], odd[k]
        if k == 0:
            tr, ti = r, i
        elif 4 * k == count:
            tr, ti = (-i, r) if sign > 0 else (i, -r)
        else:
            c = math.cos(2.0 * math.pi * k / count)
            s = sign * math.sin(2.0 * math.pi * k / count)
            if abs(abs(c) - abs(s)) < 1e-9:
                h = math.sqrt(0.5)
                sc, ss = (1 if c > 0 else -1), (1 if s > 0 else -1)
                tr = h * (r - i) if sc * ss > 0 else h * (r + i)
                ti = h * (i + r) if sc * ss > 0 else h * (i - r)
                if sc < 0:
                    tr, ti = -tr, -ti
            else:
                tr, ti = c * r - s * i, c * i + s * r
        low.append((er + tr, ei + ti))
        high.append((er - tr, ei - ti))
    return low + high


def sin_cos(angle):
    turns = jnp.round(angle * (0.5 / math.pi))
    r = angle - turns * 6.28125 - turns * (2.0 * math.pi - 6.28125)
    r2 = r * r
    s = jnp.full_like(r, 1.0 / math.factorial(17))
    for n in range(15, 0, -2):
        s = s * r2 + ((-1) ** (n // 2)) / math.factorial(n)
    c = jnp.full_like(r, -1.0 / math.factorial(18))
    for n in range(16, -1, -2):
        c = c * r2 + ((-1) ** (n // 2)) / math.factorial(n)
    return s * r, c


def split(x):
    high = x.astype(jnp.bfloat16)
    return high, (x - high.astype(jnp.float32)).astype(jnp.bfloat16)


def dot(a, b):
    return jnp.dot(a, b, preferred_element_type=jnp.float32)


def flipped(index, mask, count):
    other, bit = index, 1
    while bit < count:
        if mask & bit:
            other = other + bit * (1 - 2 * ((index // bit) % 2))
        bit *= 2
    return other


def step_kernel(
    freq_hbm, wave_hbm, src_hbm, slow_hbm, twx_hbm, tw_hbm, fwd_hbm, both_hbm, inv_hbm,
    fresh, terms_in,
    spec_out, spec_in, line_in, edge_out, edge_in, stat_out, stat_in,
    slow, terms, zs, zc, zp, ze, field, wave, source,
    twx, tw_ref, m_fwd, m_both, m_inv, freq_ref,
    wave_sem, source_sem, early_sem, late_sem, own_sem,
    slow_send, slow_recv, spec_send, spec_recv, spec_own, line_send, line_recv, line_own,
    edge_send, edge_recv, edge_own, stat_send, stat_recv, term_send, term_recv,
    *, batch_total,
):
    members, strips, rows_in, width = (spec_out.shape[i] for i in (0, 1, 3, 4))
    groups, part_width = slow.shape[0], slow.shape[2]
    full = strips * width
    factor = full // LANES
    count = rows_in * strips
    blocks, pieces = rows_in // CHUNK, rows_in // PIECE
    lane_blocks = width // LANES
    lat, fr = lax.axis_index("lat"), lax.axis_index("freq")
    lat_masks = sorted(range(1, strips), key=lambda m: -m)
    freq_masks = list(range(groups - 1, 0, -1))

    def lat_peer(mask):
        return flipped(lat, mask, strips)

    def freq_peer(mask):
        return flipped(fr, mask, groups)

    def chunk_rows(i):
        return pl.ds(pl.multiple_of(i * CHUNK, CHUNK), CHUNK)

    def piece_rows(i):
        return pl.ds(pl.multiple_of(i * PIECE, PIECE), PIECE)

    def remote(a, b, send, recv, to):
        return pltpu.make_async_remote_copy(
            src_ref=a, dst_ref=b, send_sem=send, recv_sem=recv, device_id=to, device_id_type=MESH
        )

    def wave_copy(n):
        rows = chunk_rows(n % blocks)
        return pltpu.make_async_copy(
            wave_hbm.at[:, n // blocks, rows, :], wave.at[n % 2], wave_sem.at[n % 2]
        )

    def source_copy(n):
        rows = piece_rows(n % pieces)
        return pltpu.make_async_copy(
            src_hbm.at[:, n // pieces, rows, :], source.at[n % 2], source_sem.at[n % 2]
        )

    barrier = pltpu.get_barrier_semaphore()
    for mask in freq_masks:
        pl.semaphore_signal(barrier, inc=1, device_id=(lat, freq_peer(mask)), device_id_type=MESH)
    for mask in lat_masks:
        pl.semaphore_signal(barrier, inc=1, device_id=(lat_peer(mask), fr), device_id_type=MESH)

    own_slow = pltpu.make_async_copy(slow_hbm, slow.at[fr], own_sem)
    own_slow.start()
    wave_copy(0).start()
    early = [
        pltpu.make_async_copy(a, b, early_sem.at[i])
        for i, (a, b) in enumerate(((tw_hbm, tw_ref), (fwd_hbm, m_fwd), (freq_hbm, freq_ref)))
    ]
    late = [
        pltpu.make_async_copy(a, b, late_sem.at[i])
        for i, (a, b) in enumerate(((twx_hbm, twx), (both_hbm, m_both), (inv_hbm, m_inv)))
    ]
    for copy in early:
        copy.start()
    pl.semaphore_wait(barrier, len(freq_masks) + len(lat_masks))

    def send_slow(i, carry):
        rows = chunk_rows(i)
        for mask in freq_masks:
            remote(
                slow.at[fr, rows, :], slow.at[fr, rows, :], slow_send, slow_recv.at[i],
                (lat, freq_peer(mask)),
            ).start()
        return carry

    own_slow.wait()
    lax.fori_loop(0, min(AHEAD, blocks), send_slow, 0)
    for copy in early:
        copy.wait()

    def forward(n, carry):
        m, i = n // blocks, n % blocks
        rows = chunk_rows(i)

        @pl.when(n + 1 < members * blocks)
        def _():
            wave_copy(n + 1).start()

        @pl.when(n + AHEAD < blocks)
        def _():
            send_slow(n + AHEAD, 0)

        @pl.when(n < blocks)
        def _():
            some = slow.at[pl.ds(0, groups - 1), rows, :]
            remote(some, some, slow_send, slow_recv.at[i], (lat, fr)).wait_recv()

        wave_copy(n).wait()
        scale = 2.0 * math.pi * freq_step * freq_ref[m].astype(jnp.float32) * depth_step
        slot = n % 2

        def tile(t, c0):
            r = pl.multiple_of(t * 8, 8)
            at_slow = pl.ds(pl.multiple_of(i * CHUNK + t * 8, 8), 8)
            cells = []
            for k in range(factor):
                at = k * LANES
                s = slow[at // part_width, at_slow, pl.ds(at % part_width, LANES)]
                sn, cs = sin_cos(s * scale)
                re = wave[slot, 0, pl.ds(r, 8), pl.ds(at, LANES)]
                im = wave[slot, 1, pl.ds(r, 8), pl.ds(at, LANES)]
                cells.append((re * cs - im * sn, re * sn + im * cs))
            for k, (re, im) in enumerate(fft_list(cells, -1.0)):
                if k:
                    c, s = tw_ref[0, pl.ds(k, 1), :], tw_ref[1, pl.ds(k, 1), :]
                    re, im = re * c + im * s, im * c - re * s
                zc[k, pl.ds(r, 8), pl.ds(0, LANES)] = re
                zc[k, pl.ds(r, 8), pl.ds(LANES, LANES)] = im
            return c0

        lax.fori_loop(0, CHUNK // 8, tile, 0)
        high, low = split(zc[...].reshape(factor * CHUNK, 2 * LANES))
        y = dot(high, m_fwd[0]) + (dot(low, m_fwd[0]) + dot(high, m_fwd[1]))
        y = y.reshape(factor, CHUNK, 2 * LANES)
        for k in range(factor):
            at = k * LANES
            cols = pl.ds(at % width, LANES)
            spec_out[m, at // width, 0, rows, cols] = y[k, :, :LANES]
            spec_out[m, at // width, 1, rows, cols] = y[k, :, LANES:]
        for mask in lat_masks:
            to = lat_peer(mask)
            remote(
                spec_out.at[m, to, :, rows, :], spec_in.at[m, lat, :, rows, :],
                spec_send.at[m], spec_recv.at[m, lat], (to, fr),
            ).start()
        pltpu.make_async_copy(
            spec_out.at[m, lat, :, rows, :], spec_in.at[m, lat, :, rows, :], spec_own.at[m]
        ).start()

        @pl.when(n == blocks - 1)
        def _():
            def add(t, sums):
                at_slow = pl.ds(pl.multiple_of(t * 8, 8), 8)
                for p in range(groups):
                    for at in range(0, part_width, LANES):
                        sums = sums + slow[p, at_slow, pl.ds(at, LANES)]
                return sums

            total = lax.fori_loop(0, rows_in // 8, add, jnp.zeros((8, LANES), jnp.float32))
            total = jnp.sum(total, axis=0, keepdims=True)
            stat_out[...] = total
            stat_in[lat] = total
            for mask in lat_masks:
                remote(
                    stat_out, stat_in.at[lat], stat_send, stat_recv, (lat_peer(mask), fr)
                ).start()

        return carry

    lax.fori_loop(0, members * blocks, forward, 0)

    source_copy(0).start()
    for copy in late:
        copy.start()
    some = stat_in.at[pl.ds(0, strips - 1)]
    remote(some, some, stat_send, stat_recv, (lat, fr)).wait_recv()
    for copy in late:
        copy.wait()
    mean = jnp.sum(stat_in[...]) * (1.0 / (count * full))

    def shift(m, carry):
        own = spec_in.at[m, lat]
        pltpu.make_async_copy(own, own, spec_own.at[m]).wait()
        for mask in lat_masks:
            peer = lat_peer(mask)
            whole_in = spec_in.at[m, peer]
            remote(whole_in, whole_in, spec_send.at[m], spec_recv.at[m, peer], (lat, fr)).wait_recv()

        def tile_in(t, c0):
            r = pl.multiple_of(t * 8, 8)
            for lane in range(0, width, LANES):
                lanes = pl.ds(lane, LANES)
                cells = []
                for n in range(factor):
                    at = n * LANES
                    rows = pl.ds(at % rows_in + r, 8)
                    cells.append(
                        (spec_in[m, at // rows_in, 0, rows, lanes],
                         spec_in[m, at // rows_in, 1, rows, lanes])
                    )
                for k, (re, im) in enumerate(fft_list(cells, -1.0)):
                    if k:
                        c, s = twx[0, k, pl.ds(r, 8), :], twx[1, k, pl.ds(r, 8), :]
                        re, im = re * c + im * s, im * c - re * s
                    zs[k, pl.ds(r, 8), lanes] = re
                    zs[k, pl.ds(LANES + r, 8), lanes] = im
            return c0

        lax.fori_loop(0, LANES // 8, tile_in, 0)

        angular_mean = 2.0 * math.pi * freq_step * freq_ref[m].astype(jnp.float32) * mean
        flat = angular_mean * depth_step
        place = lat * width + lax.broadcasted_iota(jnp.int32, (LANES, width), 1)
        index_y = place // LANES + factor * (place % LANES)
        signed_y = jnp.where(index_y < full // 2, index_y, index_y - full)
        wave_y = 2.0 * math.pi / (full * grid_step) * signed_y.astype(jnp.float32)
        rest = angular_mean * angular_mean - wave_y * wave_y
        row = lax.broadcasted_iota(jnp.int32, (LANES, width), 0)

        def product(k, c0):
            high, low = split(zs[k])
            y = dot(m_both[0], high) + (dot(m_both[0], low) + dot(m_both[1], high))
            index_x = k + factor * row
            signed_x = jnp.where(index_x < count // 2, index_x, index_x - count)
            wave_x = 2.0 * math.pi / (count * grid_step) * signed_x.astype(jnp.float32)
            vertical = rest - wave_x * wave_x
            size = jnp.sqrt(jnp.abs(vertical)) * depth_step
            damping = jnp.where(vertical < 0.0, jnp.exp(-size), 1.0) * (1.0 / (count * full))
            sn, cs = sin_cos(jnp.where(vertical > 0.0, size, 0.0) - flat)
            tr, ti = damping * cs, damping * sn
            re, im = y[:LANES], y[LANES:]
            z = jnp.concatenate([re * tr - im * ti, re * ti + im * tr], axis=0)
            high, low = split(z)
            zs[k] = dot(m_both[2], high) + (dot(m_both[2], low) + dot(m_both[3], high))
            return c0

        lax.fori_loop(0, factor, product, 0)
        some = spec_out.at[m, pl.ds(0, strips - 1)]
        remote(some, some, spec_send.at[m], spec_recv.at[m, 0], (lat, fr)).wait_send()

        def tile_out(t, c0):
            r = pl.multiple_of(t * 8, 8)
            for lane in range(0, width, LANES):
                lanes = pl.ds(lane, LANES)
                cells = []
                for k in range(factor):
                    re, im = zs[k, pl.ds(r, 8), lanes], zs[k, pl.ds(LANES + r, 8), lanes]
                    if k:
                        c, s = twx[0, k, pl.ds(r, 8), :], twx[1, k, pl.ds(r, 8), :]
                        re, im = re * c - im * s, im * c + re * s
                    cells.append((re, im))
                for n, (re, im) in enumerate(fft_list(cells, 1.0)):
                    at = n * LANES
                    rows = pl.ds(at % rows_in + r, 8)
                    spec_out[m, at // rows_in, 0, rows, lanes] = re
                    spec_out[m, at // rows_in, 1, rows, lanes] = im
            return c0

        lax.fori_loop(0, LANES // 8, tile_out, 0)

        for d in range(strips):
            for c in range(2):
                for e in range(2):
                    beside = d - 1 if e == 0 else d + 1
                    at_row = rows_in - 1 if e == 0 else 0
                    for b in range(lane_blocks):
                        if 0 <= beside < strips:
                            value = spec_out[m, beside, c, pl.ds(at_row, 1), pl.ds(b * LANES, LANES)]
                        else:
                            value = jnp.zeros((1, LANES), jnp.float32)
                        at = (c * 2 + e) * lane_blocks + b
                        edge_out[m, d, pl.ds(at, 1), :] = value

        for mask in lat_masks:
            to = lat_peer(mask)
            remote(
                edge_out.at[m, to], edge_in.at[m, lat], edge_send.at[m], edge_recv.at[m], (to, fr)
            ).start()
        pltpu.make_async_copy(edge_out.at[m, lat], edge_in.at[m, lat], edge_own.at[m]).start()

        def send_lines(i, c0):
            rows = piece_rows(i)
            for mask in lat_masks:
                to = lat_peer(mask)
                remote(
                    spec_out.at[m, to, :, rows, :], line_in.at[m, lat, :, rows, :],
                    line_send.at[m], line_recv.at[m, i], (to, fr),
                ).start()
            pltpu.make_async_copy(
                spec_out.at[m, lat, :, rows, :], line_in.at[m, lat, :, rows, :], line_own.at[m, i]
            ).start()
            return c0

        lax.fori_loop(0, pieces, send_lines, 0)
        return carry

    lax.fori_loop(0, members, shift, 0)

    def columns(z, rows):
        cells = []
        for k in range(factor):
            re, im = z[k, rows, pl.ds(0, LANES)], z[k, rows, pl.ds(LANES, LANES)]
            if k:
                c, s = tw_ref[0, pl.ds(k, 1), :], tw_ref[1, pl.ds(k, 1), :]
                re, im = re * c - im * s, im * c + re * s
            cells.append((re, im))
        return fft_list(cells, 1.0)

    def inverse_dot(x):
        high, low = split(x)
        return dot(high, m_inv[0]) + (dot(low, m_inv[0]) + dot(high, m_inv[1]))

    def edges(m):
        own = edge_in.at[m, lat]
        pltpu.make_async_copy(own, own, edge_own.at[m]).wait()
        some = edge_in.at[m, pl.ds(0, strips - 1)]
        remote(some, some, edge_send.at[m], edge_recv.at[m], (lat, fr)).wait_recv()
        ze[...] = jnp.zeros_like(ze)
        for k in range(factor):
            at = k * LANES
            b = (at % width) // LANES
            for c in range(2):
                for e in range(2):
                    row_at = (c * 2 + e) * lane_blocks + b
                    ze[k, pl.ds(e, 1), pl.ds(c * LANES, LANES)] = edge_in[
                        m, at // width, pl.ds(row_at, 1), :
                    ]
        y = inverse_dot(ze[...].reshape(factor * 8, 2 * LANES))
        ze[...] = y.reshape(factor, 8, 2 * LANES)
        for n, pair in enumerate(columns(ze, pl.ds(0, 8))):
            for c in range(2):
                field[c, pl.ds(7, 1), pl.ds(n * LANES, LANES)] = pair[c][0:1]
                field[c, pl.ds(8 + rows_in, 1), pl.ds(n * LANES, LANES)] = pair[c][1:2]

    def inverse_block(m, i):
        rows = piece_rows(i)
        own = line_in.at[m, lat, :, rows, :]
        pltpu.make_async_copy(own, own, line_own.at[m, i]).wait()
        some = line_in.at[m, pl.ds(0, strips - 1), :, rows, :]
        remote(some, some, line_send.at[m], line_recv.at[m, i], (lat, fr)).wait_recv()
        parts = []
        for k in range(factor):
            at = k * LANES
            cols = pl.ds(at % width, LANES)
            parts.append(
                jnp.concatenate(
                    [line_in[m, at // width, 0, rows, cols], line_in[m, at // width, 1, rows, cols]],
                    axis=1,
                )
            )
        y = inverse_dot(jnp.concatenate(parts, axis=0))
        zp[...] = y.reshape(factor, PIECE, 2 * LANES)

        def tile(t, c0):
            r = pl.multiple_of(t * 8, 8)
            at_field = pl.ds(pl.multiple_of(8 + i * PIECE + t * 8, 8), 8)
            for n, pair in enumerate(columns(zp, pl.ds(r, 8))):
                for c in range(2):
                    field[c, at_field, pl.ds(n * LANES, LANES)] = pair[c]
            return c0

        lax.fori_loop(0, PIECE // 8, tile, 0)

    column = lax.broadcasted_iota(jnp.int32, (PIECE, full), 1)

    def stencil(m, i):
        n = m * pieces + i
        slot = n % 2
        rows = piece_rows(i)

        @pl.when(n + 1 < members * pieces)
        def _():
            source_copy(n + 1).start()

        source_copy(n).wait()
        angular = 2.0 * math.pi * freq_step * freq_ref[m].astype(jnp.float32)
        ahead = 0.5 / (angular * mean)
        start = pl.multiple_of(i * PIECE, PIECE)
        centre, laplace = [], []
        for c in range(2):
            cells = field[c, pl.ds(start, PIECE + 16), :]
            mid = cells[8 : 8 + PIECE]
            up = pltpu.roll(cells, 1, 0)[8 : 8 + PIECE]
            down = pltpu.roll(cells, PIECE + 15, 0)[8 : 8 + PIECE]
            left = jnp.where(column == 0, 0.0, pltpu.roll(mid, 1, 1))
            right = jnp.where(column == full - 1, 0.0, pltpu.roll(mid, full - 1, 1))
            centre.append(mid)
            laplace.append(up + down + left + right - 4.0 * mid)
        slow_rows = jnp.concatenate([slow[p, rows, :] for p in range(groups)], axis=1)
        gain = (ahead - 0.5 / (angular * slow_rows)) * (depth_step / (grid_step * grid_step))
        new_re = centre[0] + gain * laplace[1]
        new_im = centre[1] - gain * laplace[0]
        fresh[0, m, rows, :] = new_re
        fresh[1, m, rows, :] = new_im
        term = (new_re * source[slot, 0] + new_im * source[slot, 1]) * (
            1.0 / math.sqrt(batch_total)
        )
        for p in range(groups):
            part = term[:, p * part_width : (p + 1) * part_width]

            @pl.when(m == 0)
            def _():
                terms[p, rows, :] = part

            @pl.when(m > 0)
            def _():
                terms[p, rows, :] = terms[p, rows, :] + part

        @pl.when(m == members - 1)
        def _():
            for mask in freq_masks:
                to = freq_peer(mask)
                remote(
                    terms.at[to, rows, :], terms_in.at[fr, rows, :], term_send, term_recv,
                    (lat, to),
                ).start()
            terms_in[fr, rows, :] = terms[fr, rows, :]

    def finish(n, carry):
        m, j = n // (pieces + 1), n % (pieces + 1)

        @pl.when(j == 0)
        def _():
            edges(m)

        @pl.when(j < pieces)
        def _():
            inverse_block(m, j)

        @pl.when(j > 0)
        def _():
            stencil(m, j - 1)

        return carry

    lax.fori_loop(0, members * (pieces + 1), finish, 0)
    some = slow.at[pl.ds(0, groups - 1)]
    remote(some, some, slow_send, slow_recv.at[0], (lat, fr)).wait_send()
    some = terms.at[pl.ds(0, groups - 1)]
    remote(some, some, term_send, term_recv, (lat, fr)).wait()
    some = stat_in.at[pl.ds(0, strips - 1)]
    remote(some, some, stat_send, stat_recv, (lat, fr)).wait_send()
    for m in range(members):
        some = spec_out.at[m, pl.ds(0, strips - 1)]
        remote(some, some, line_send.at[m], line_recv.at[m, 0], (lat, fr)).wait_send()
        some = edge_out.at[m, pl.ds(0, strips - 1)]
        remote(some, some, edge_send.at[m], edge_recv.at[m], (lat, fr)).wait_send()


def write_kernel(fresh, terms, field_hbm, image_hbm, image, field_sem, image_sem):
    rows = fresh.shape[2]
    part = rows // 4
    for r in range(0, rows, part):
        for c in range(fresh.shape[0]):
            for m in range(fresh.shape[1]):
                pltpu.make_async_copy(
                    fresh.at[c, m, pl.ds(r, part)], field_hbm.at[c, m, pl.ds(r, part)], field_sem
                ).start()
    total = terms[0]
    for p in range(1, terms.shape[0]):
        total = total + terms[p]
    image[...] = total
    copy = pltpu.make_async_copy(image, image_hbm, image_sem)
    copy.start()
    copy.wait()
    pltpu.make_async_copy(fresh, field_hbm, field_sem).wait()


def local(wavefield, source_field, slowness, freq_index):
    _, members, rows, full = wavefield.shape
    strips, groups = lax.axis_size("lat"), lax.axis_size("freq")
    width = full // strips
    factor = full // LANES
    part_width = full // groups
    blocks, pieces = rows // CHUNK, rows // PIECE
    tw = twiddle(full)
    tw_row = jnp.asarray(tw)
    tw_x = jnp.asarray(np.ascontiguousarray(np.broadcast_to(tw[..., None], tw.shape + (LANES,))))
    right_fwd, right_inv = dft_tables(-1.0), dft_tables(1.0)
    m_fwd, m_inv = split_table(right_fwd), split_table(right_inv)
    m_both = jnp.concatenate(
        [split_table(np.ascontiguousarray(right_fwd.T)), split_table(np.ascontiguousarray(right_inv.T))]
    )
    edge_rows = max(8, 4 * width // LANES)
    far = pl.BlockSpec(memory_space=pltpu.HBM)
    anywhere = pl.BlockSpec(memory_space=pl.ANY)
    inside = pl.BlockSpec(memory_space=pltpu.VMEM)
    f32 = jnp.float32
    dma = pltpu.SemaphoreType.DMA
    fresh, terms = pl.pallas_call(
        functools.partial(step_kernel, batch_total=members * groups),
        in_specs=[far] * 9,
        out_specs=[inside, inside],
        out_shape=[
            pltpu.VMEM((2, members, rows, full), f32),
            pltpu.VMEM((groups, rows, part_width), f32),
        ],
        scratch_shapes=[
            pltpu.VMEM((members, strips, 2, rows, width), f32),
            pltpu.VMEM((members, strips, 2, rows, width), f32),
            pltpu.VMEM((members, strips, 2, rows, width), f32),
            pltpu.VMEM((members, strips, edge_rows, LANES), f32),
            pltpu.VMEM((members, strips, edge_rows, LANES), f32),
            pltpu.VMEM((1, LANES), f32),
            pltpu.VMEM((strips, 1, LANES), f32),
            pltpu.VMEM((groups, rows, part_width), f32),
            pltpu.VMEM((groups, rows, part_width), f32),
            pltpu.VMEM((factor, 2 * LANES, width), f32),
            pltpu.VMEM((factor, CHUNK, 2 * LANES), f32),
            pltpu.VMEM((factor, PIECE, 2 * LANES), f32),
            pltpu.VMEM((factor, 8, 2 * LANES), f32),
            pltpu.VMEM((2, rows + 16, full), f32),
            pltpu.VMEM((2, 2, CHUNK, full), f32),
            pltpu.VMEM((2, 2, PIECE, full), f32),
            pltpu.VMEM(tw_x.shape, f32),
            pltpu.VMEM(tw_row.shape, f32),
            pltpu.VMEM(m_fwd.shape, m_fwd.dtype),
            pltpu.VMEM(m_both.shape, m_both.dtype),
            pltpu.VMEM(m_inv.shape, m_inv.dtype),
            pltpu.SMEM((members,), jnp.int32),
            dma((2,)), dma((2,)), dma((3,)), dma((3,)), dma,
            dma, dma((blocks,)),
            dma((members,)), dma((members, strips)), dma((members,)),
            dma((members,)), dma((members, pieces)), dma((members, pieces)),
            dma((members,)), dma((members,)), dma((members,)),
            dma, dma,
            dma, dma,
        ],
        compiler_params=pltpu.CompilerParams(
            collective_id=0, has_side_effects=True, vmem_limit_bytes=VMEM_BYTES
        ),
        cost_estimate=pl.CostEstimate(
            flops=13_000_000_000, bytes_accessed=26_000_000, transcendentals=0
        ),
        name="depth_step",
    )(freq_index, wavefield, source_field, slowness, tw_x, tw_row, m_fwd, m_both, m_inv)
    return pl.pallas_call(
        write_kernel,
        in_specs=[inside, inside],
        out_specs=[anywhere, anywhere],
        out_shape=[
            jax.ShapeDtypeStruct((2, members, rows, full), f32),
            jax.ShapeDtypeStruct((rows, part_width), f32),
        ],
        scratch_shapes=[pltpu.VMEM((rows, part_width), f32), dma, dma],
        compiler_params=pltpu.CompilerParams(vmem_limit_bytes=SMALL_BYTES),
        cost_estimate=pl.CostEstimate(flops=400_000, bytes_accessed=8_400_000, transcendentals=0),
        name="write_out",
    )(fresh, terms)


def solution(mesh):
    return jax.shard_map(
        local,
        mesh=mesh,
        in_specs=(
            P(None, "freq", "lat", None),
            P(None, "freq", "lat", None),
            P("lat", "freq"),
            P("freq"),
        ),
        out_specs=(P(None, "freq", "lat", None), P("lat", "freq")),
        check_vma=False,
    )
```
